256 devices in a mesh: seq: 32 (over y, x, core), dp: 8 (over z).
Axes of the slice: x: 4, y: 4, z: 8, core: 2. Of those that a mesh axis runs over, the one named last changes fastest.
Arguments:
- mixer_input: bfloat16 [8, 8192, 2560], P('dp', 'seq'), may hold values from -6 to 6
- scan_input: bfloat16 [8, 8192, 2560], P('dp', 'seq'), may hold values from -6 to 6
- step_logits: float32 [8, 40, 8192], P('dp', None, 'seq'), may hold values from -2 to 5
- output_grad: bfloat16 [8, 8192, 2560], P('dp', 'seq'), may hold values from -6 to 6
- state_proj: bfloat16 [2560, 256], replicated, may hold values from -0.125 to 0.125
- step_bias: float32 [40], replicated, may hold values from -6 to -4
- rate_log: float32 [40], replicated, may hold values from -10 to 2
- direct_coefficient: float32 [40], replicated, may hold values from 0.5 to 1.5
Outputs:
- scan_grad: bfloat16 [8, 8192, 2560], P('dp', 'seq')
- logit_grad: float32 [8, 40, 8192], P('dp', None, 'seq')
- mixer_grad: bfloat16 [8, 8192, 2560], P('dp', 'seq')
- proj_grad: float32 [2560, 256], P('seq')
- rate_grad: float32 [40], replicated
- skip_grad: float32 [40], replicated
- bias_grad: float32 [40], replicated
The draws below stay inside these ranges and needn't reach their ends.
All inputs are finite; a program needn't handle non-finite values.
Results may differ from the reference program's by a relative error of at most 0.0065.
Values sent between devices are 32-bit elements; how exact they have to be, the bound alone decides.
No kernel may reach another device: no remote copies, remote signals or barrier semaphores. Data moves between devices by JAX's collectives and lax.ppermute only.
A program may use at most 256 MiB of HBM per device.

```python
import math
from functools import partial
import jax
import jax.numpy as jnp
from jax import lax

D = 2560
H = 40
P_SIZE = 64
N = 128
TOK_DEV = 256
LENGTH = 8192
REPLICAS = 8


def draw_step_logits(key, part):
    key = jax.random.fold_in(key, 11)
    rough_key, level_key, slot_key = jax.random.split(key, 3)
    block_count = LENGTH // TOK_DEV
    quick_blocks = jax.random.randint(level_key, (REPLICAS, H, block_count), 0, 4) == 0
    block_level = jnp.where(quick_blocks, 2.5, -1.7).astype(jnp.float32)
    level = jnp.repeat(block_level, TOK_DEV, axis=2)
    rough = jnp.clip(0.3 * jax.random.normal(rough_key, (REPLICAS, H, LENGTH), jnp.float32), -0.9, 0.9)
    sequence_slots = jax.random.randint(slot_key, (REPLICAS, 6), 0, LENGTH)
    element_ordinals = jnp.arange(LENGTH)
    segment_bundles = jnp.any(element_ordinals[None, :, None] == sequence_slots[:, None, :], axis=2)
    raised = level + rough + 3.0 * segment_bundles.astype(jnp.float32)[:, None, :]
    return jnp.clip(raised, -2.0, 5.0)


def draw_rate_log(key, part):
    lowest = math.log(60.0 / LENGTH)
    highest = math.log(4.0)
    return jax.random.uniform(jax.random.fold_in(key, 23), (H,), jnp.float32, lowest, highest)


def steps_of(own_key, extent, cuts, low, high):
    level = 1.0
    for dim, blocks in cuts:
        draws = jax.random.uniform(jax.random.fold_in(jax.random.fold_in(own_key, 6), dim), (blocks,), jnp.float32, low / len(cuts), high / len(cuts))
        level = level * jnp.repeat(jnp.exp(draws), extent[dim] // blocks).reshape((-1,) + (1,) * (len(extent) - 1 - dim))
    return level


def gaussian(stream_key, extent, deviation, most, cuts=(), kind=jnp.bfloat16):
    drawn = jax.random.normal(stream_key, extent, jnp.float32) * deviation
    if len(cuts) > 0:
        drawn = steps_of(stream_key, extent, cuts, -0.22, 0.18) * drawn
    return jnp.clip(drawn, min=-most, max=most).astype(kind)


def setup_inputs(seed: int = 0) -> dict:
    streams_of = jax.random.split(jax.random.key(seed), 9)
    mixer_input = gaussian(streams_of[0], (REPLICAS, LENGTH, D), 1.0, 6.0, ((0, 8), (1, 32)))
    scan_input = gaussian(streams_of[1], (REPLICAS, LENGTH, H * P_SIZE), 1.0, 6.0, ((0, 8), (1, 32)))
    step_logits = draw_step_logits(jax.random.fold_in(streams_of[8], 71), 0)
    output_grad = gaussian(streams_of[3], (REPLICAS, LENGTH, H * P_SIZE), 1.0, 6.0, ((0, 8), (1, 32)))
    state_proj = gaussian(streams_of[4], (D, 2 * N), D ** -0.5, 0.125)
    step_bias = jnp.clip(jax.random.uniform(streams_of[5], (H,), jnp.float32, -6.0, -4.0), -6.0, -4.0)
    rate_log = draw_rate_log(jax.random.fold_in(streams_of[8], 71), 0)
    direct_coefficient = jnp.clip(jax.random.uniform(streams_of[7], (H,), jnp.float32, 0.5, 1.5), 0.5, 1.5)
    return {"mixer_input": mixer_input, "scan_input": scan_input, "step_logits": step_logits, "output_grad": output_grad, "state_proj": state_proj, "step_bias": step_bias, "rate_log": rate_log, "direct_coefficient": direct_coefficient}


exact_precision = lax.Precision.HIGHEST

def block_step(rate, state, inputs):
    x_block, dt_block, b_block, c_block = inputs
    log_decay = jnp.cumsum(-rate[:, None] * dt_block, axis=1)
    block_len = dt_block.shape[1]
    causal_mask = jnp.arange(block_len)[:, None] >= jnp.arange(block_len)[None, :]
    log_gap = log_decay[:, :, None] - log_decay[:, None, :]
    decay = jnp.where(causal_mask[None], jnp.exp(jnp.where(causal_mask[None], log_gap, 0.0)), 0.0)
    scores = jnp.dot(c_block, b_block.T, precision=exact_precision)
    x_scaled = x_block * dt_block.T[:, :, None]
    within = jnp.einsum('hts,shp->thp', decay * scores[None], x_scaled, precision=exact_precision)
    carried = jnp.exp(log_decay).T[:, :, None] * jnp.einsum('tn,hpn->thp', c_block, state, precision=exact_precision)
    final_log = log_decay[:, -1]
    weights = jnp.exp(final_log[:, None] - log_decay)
    new_state = jnp.exp(final_log)[:, None, None] * state + jnp.einsum('hs,shp,sn->hpn', weights, x_scaled, b_block, precision=exact_precision)
    return (new_state, within + carried)

def forward(flattened_input, logits, bc_float, bias, rate_log, direct_coefficient):
    length = flattened_input.shape[0]
    head_count = logits.shape[0]
    head_dim = flattened_input.shape[1] // head_count
    state_dim = bc_float.shape[1] // 2
    block_len = 128 if length % 128 == 0 else length
    block_count = length // block_len
    step_dt = jax.nn.softplus(logits + bias[:, None])
    rate = jnp.exp(rate_log)
    x_blocks = flattened_input.reshape(block_count, block_len, head_count, head_dim)
    dt_blocks = step_dt.reshape(head_count, block_count, block_len).transpose(1, 0, 2)
    b_blocks = bc_float[:, :state_dim].reshape(block_count, block_len, state_dim)
    c_blocks = bc_float[:, state_dim:].reshape(block_count, block_len, state_dim)
    stepper = jax.checkpoint(partial(block_step, rate))
    start = jnp.zeros((head_count, head_dim, state_dim), jnp.float32)
    _, outputs = lax.scan(stepper, start, (x_blocks, dt_blocks, b_blocks, c_blocks))
    return outputs.reshape(length, head_count * head_dim) + jnp.repeat(direct_coefficient, head_dim)[None, :] * flattened_input

def one_replica(state_proj, step_bias, rate_log, direct_coefficient, inputs):
    tokens, x_in, logits, grads_in = inputs
    bc_round = jnp.dot(tokens, state_proj, preferred_element_type=jnp.float32).astype(jnp.bfloat16)
    _, pullback = jax.vjp(forward, x_in.astype(jnp.float32), logits, bc_round.astype(jnp.float32), step_bias, rate_log, direct_coefficient)
    grad_x, grad_logit, grad_bc, grad_bias, grad_rate, grad_skip = pullback(grads_in.astype(jnp.float32))
    state_grad = grad_bc.astype(jnp.bfloat16)
    mixer = lax.dot_general(state_grad, state_proj, (((1,), (1,)), ((), ())), preferred_element_type=jnp.float32).astype(jnp.bfloat16)
    weight = lax.dot_general(tokens, state_grad, (((0,), (0,)), ((), ())), preferred_element_type=jnp.float32)
    return (grad_x.astype(jnp.bfloat16), grad_logit, mixer, weight, grad_rate, grad_skip, grad_bias)

def reference(mixer_input, scan_input, step_logits, output_grad, state_proj, step_bias, rate_log, direct_coefficient):
    results = lax.map(partial(one_replica, state_proj, step_bias, rate_log, direct_coefficient), (mixer_input, scan_input, step_logits, output_grad))
    grad_scale = float(REPLICAS * LENGTH) ** (-0.5)
    scan_grad, logit_grad, mixer_grad, weights, rates, skips, biases = results
    proj_grad = lax.optimization_barrier(jnp.sum(weights, axis=0)) * grad_scale
    return (scan_grad, logit_grad, mixer_grad, proj_grad, lax.optimization_barrier(jnp.sum(rates, axis=0)) * grad_scale, lax.optimization_barrier(jnp.sum(skips, axis=0)) * grad_scale, lax.optimization_barrier(jnp.sum(biases, axis=0)) * grad_scale)
```

```python
from functools import partial

import jax
import jax.numpy as jnp
from jax import lax
from jax.sharding import PartitionSpec as P
import jax.experimental.pallas as pl
import jax.experimental.pallas.tpu as pltpu

f32 = jnp.float32
bf16 = jnp.bfloat16

T = 256
H = 40
HD = 64
W = 2560
N = 128
HALF = 64
TAIL = 128
CHIPS = 16
ROWS = 80
PROWS = 88


def iota(shape, dim):
    return lax.broadcasted_iota(jnp.int32, shape, dim)


def split3(v):
    hi = v.astype(bf16).astype(f32)
    rest = v - hi
    mid = rest.astype(bf16).astype(f32)
    return hi, mid, rest - mid


def dot00(a, b):
    return lax.dot_general(a, b, (((0,), (0,)), ((), ())), preferred_element_type=f32)


def dot11(a, b):
    return lax.dot_general(a, b, (((1,), (1,)), ((), ())), preferred_element_type=f32)


def dot10(a, b):
    return lax.dot_general(a, b, (((1,), (0,)), ((), ())), preferred_element_type=f32)


def head_rows(count):
    lane_head = iota((count, W), 1) >> 6
    row = iota((count, W), 0)
    hit = (lane_head == row) | (lane_head == row - H) | (lane_head == row - 2 * H)
    return jnp.where(hit, 1.0, 0.0).astype(bf16)


def widen(v, spread):
    parts = jnp.concatenate(split3(v) + (jnp.zeros((8, T), f32),), axis=0).astype(bf16)
    return dot00(parts, spread)


def widen_row(row, spread):
    parts = jnp.concatenate(split3(row) + (jnp.zeros((8, 128), f32),), axis=0).astype(bf16)
    lanes = iota((N, W), 0) < H
    once = jnp.where(lanes, spread.astype(f32), 0.0).astype(bf16)
    out = dot10(parts, once)
    return out[0:8] + out[8:16] + out[16:24]


def column(row, count):
    eye = iota((count, count), 0) == iota((count, count), 1)
    return jnp.sum(jnp.where(eye, row, 0.0), axis=1, keepdims=True)


def over_positions(v, keep):
    parts = jnp.concatenate(split3(v) + (jnp.zeros((8, T), f32),), axis=0).astype(bf16)
    out = dot10(parts, jnp.where(keep, 1.0, 0.0).astype(bf16))
    return out[0:H] + out[H : 2 * H] + out[2 * H : 3 * H]


def step_sizes(logits, bias_row):
    z = logits + column(bias_row, H)
    e = jnp.exp(-jnp.abs(z))
    r = e / (2.0 + e)
    r2 = r * r
    poly = 1.0 / 17.0
    for odd in (15, 13, 11, 9, 7, 5, 3):
        poly = poly * r2 + 1.0 / odd
    dt = jnp.maximum(z, 0.0) + 2.0 * (r + r * r2 * poly)
    sig = jnp.where(z >= 0.0, 1.0, e) / (1.0 + e)
    return dt, sig


def summary_kernel(
    core_ref, tok_ref, x_ref, g_ref, proj_ref, logit_ref, bias_ref, rate_ref,
    bc_ref, xw_ref, ge_ref, keep_ref, send_ref, log_ref, dt_ref, sig_ref,
    both,
):
    bc = dot10(tok_ref[...], proj_ref[...]).astype(bf16)
    bc_ref[...] = bc
    dt, sig = step_sizes(logit_ref[...], bias_ref[...])
    rate = jnp.exp(column(rate_ref[...], H))
    log_decay = over_positions(-rate * dt, iota((T, T), 0) <= iota((T, T), 1))
    last = log_decay[:, T - 1 : T]
    log_ref[...] = log_decay
    dt_ref[...] = dt
    sig_ref[...] = sig
    spread = head_rows(N)
    xw = (x_ref[...].astype(f32) * widen(jnp.exp(last - log_decay) * dt, spread)).astype(bf16)
    xw_ref[...] = xw
    ge = (g_ref[...].astype(f32) * widen(jnp.exp(log_decay), spread)).astype(bf16)
    ge_ref[...] = ge
    both[0:N, :] = dot00(bc[:, :N], xw)
    both[N : 2 * N, :] = dot00(bc[:, N:], ge)
    mine = pl.multiple_of(core_ref[0] * HALF, HALF)
    theirs = pl.multiple_of(HALF - core_ref[0] * HALF, HALF)
    keep_ref[0:HALF, 0:W] = both[pl.ds(mine, HALF), :]
    keep_ref[HALF:N, 0:W] = both[pl.ds(N + mine, HALF), :]
    send_ref[0:HALF, 0:W] = both[pl.ds(theirs, HALF), :]
    send_ref[HALF:N, 0:W] = both[pl.ds(N + theirs, HALF), :]
    on_lane = iota((H, TAIL), 0) == iota((H, TAIL), 1)
    decay = jnp.exp(jnp.sum(jnp.where(on_lane, last, 0.0), axis=0, keepdims=True))
    decay = jnp.broadcast_to(decay, (N, TAIL))
    keep_ref[:, W:] = decay
    send_ref[:, W:] = decay


def chip_kernel(core_ref, keep_ref, got_ref, out_ref):
    spread = head_rows(N)
    decay_mine = keep_ref[0:8, W:]
    decay_their = got_ref[0:8, W:]
    wide_mine = widen_row(decay_mine, spread)[0:1]
    wide_their = widen_row(decay_their, spread)[0:1]
    first = core_ref[0] == 0
    one = jnp.ones((1, W), f32)
    a = jnp.where(first, wide_their, one)
    b = jnp.where(first, one, wide_mine)
    c = jnp.where(first, one, wide_their)
    d = jnp.where(first, wide_mine, one)
    out_ref[0:HALF, 0:W] = a * keep_ref[0:HALF, 0:W] + b * got_ref[0:HALF, 0:W]
    out_ref[HALF:N, 0:W] = c * keep_ref[HALF:N, 0:W] + d * got_ref[HALF:N, 0:W]
    out_ref[:, W:] = keep_ref[:, W:] * got_ref[:, W:]


def scan_kernel(back_ref, in_ref, after_ref, out_ref, wide):
    spread = head_rows(N)
    for c in range(CHIPS):
        wide[c] = widen_row(in_ref[c, :, W:], spread)
    back = back_ref[0]
    state = jnp.zeros((8, W), f32)
    for i in range(CHIPS):
        c = jnp.where(back == 1, CHIPS - 1 - i, i)
        out_ref[c] = state
        state = wide[c] * state + in_ref[c, :, 0:W]


def core_kernel(core_ref, chip_ref, keep_ref, got_ref, mine_ref, send_ref):
    spread = head_rows(N)
    wide_mine = widen_row(keep_ref[0:8, W:], spread)[0:1]
    wide_their = widen_row(got_ref[0:8, W:], spread)[0:1]
    s = chip_ref[0:HALF, :]
    e = chip_ref[HALF:N, :]

    @pl.when(core_ref[0] == 0)
    def _():
        mine_ref[0:HALF, :] = s
        mine_ref[HALF:N, :] = wide_their * e + got_ref[HALF:N, 0:W]
        send_ref[0:HALF, :] = wide_mine * s + keep_ref[0:HALF, 0:W]
        send_ref[HALF:N, :] = e

    @pl.when(core_ref[0] == 1)
    def _():
        mine_ref[0:HALF, :] = wide_their * s + got_ref[0:HALF, 0:W]
        mine_ref[HALF:N, :] = e
        send_ref[0:HALF, :] = s
        send_ref[HALF:N, :] = wide_mine * e + keep_ref[HALF:N, 0:W]


def within_kernel(
    tok_ref, x_ref, g_ref, bc_ref, log_ref, dt_ref,
    du_ref, sg_ref, cross_ref, col_ref, skip_ref, tokt_ref,
    wide_log, late_log, ds, rows,
):
    half = T // 2
    spread = head_rows(N)
    log_decay = log_ref[...]
    dt = dt_ref[...]
    wide_log[...] = widen(log_decay, spread)
    late_log[...] = log_decay - jnp.log(dt)
    b = bc_ref[:, :N]
    c = bc_ref[:, N:]
    scores = dot11(c, b)
    ds[...] = jnp.zeros((T, T), f32)
    rows[...] = jnp.zeros((T, 128), f32)
    causal = iota((half, half), 0) >= iota((half, half), 1)
    lane = iota((T, 128), 1)

    def pair(i, carry):
        cols = pl.ds(pl.multiple_of(i * 128, 128), 128)
        xp = x_ref[:, cols]
        gp = g_ref[:, cols]
        logs = wide_log[:, cols]
        total = jnp.zeros((T, 128), f32)
        for m in range(2):
            h = 2 * i + m
            gm = jnp.where((lane >= HD) == (m == 1), gp.astype(f32), 0.0).astype(bf16)
            q0 = dot11(gm[0:half], xp[0:half])
            q1 = dot11(gm[half:], xp)
            late = late_log[pl.ds(h, 1), :]
            lc = logs[:, m * HD : m * HD + 1]
            gap0 = lc[0:half] - late[:, 0:half]
            gap1 = lc[half:] - late[:, half:]
            dec0 = jnp.exp(jnp.where(causal, gap0, -1e30))
            dec1 = jnp.concatenate(
                [
                    jnp.exp(lc[half:] - late[:, 0:half]),
                    jnp.exp(jnp.where(causal, gap1, -1e30)),
                ],
                axis=1,
            )
            m0 = dec0 * scores[0:half, 0:half]
            m1 = dec1 * scores[half:, :]
            ds[0:half, 0:half] += dec0 * q0
            ds[half:, :] += dec1 * q1
            p0 = m0 * q0
            p1 = m1 * q1
            rsum = jnp.concatenate(
                [jnp.sum(p0, axis=1, keepdims=True), jnp.sum(p1, axis=1, keepdims=True)], axis=0
            )
            rows[...] += jnp.where(lane == h, rsum, 0.0)
            csum1 = jnp.sum(p1, axis=0, keepdims=True)
            csum0 = jnp.sum(p0, axis=0, keepdims=True)
            col_ref[pl.ds(h, 1), :] = csum1 + jnp.concatenate(
                [csum0, jnp.zeros((1, half), f32)], axis=1
            )
            m1b = m1.astype(bf16)
            early = dot00(m0.astype(bf16), gm[0:half])
            both = dot00(m1b, gm[half:])
            total = total + both + jnp.concatenate([early, jnp.zeros((half, 128), f32)], axis=0)
        du_ref[:, cols] = total
        return carry

    lax.fori_loop(0, H // 2, pair, 0)
    hi, mid, _ = split3(ds[...])
    hi = hi.astype(bf16)
    mid = mid.astype(bf16)
    sg_ref[:, :N] = dot00(hi, c) + dot00(mid, c)
    sg_ref[:, N:] = dot10(hi, b) + dot10(mid, b)
    cross_ref[...] = rows[...].T[0:H, :] - col_ref[...]
    xg = x_ref[...].astype(f32) * g_ref[...].astype(f32)
    part = jnp.sum(xg.reshape(T // 8, 8, W), axis=0)
    skip = dot11(jnp.concatenate(split3(part), axis=0).astype(bf16), spread)
    skip = jnp.sum(skip, axis=0, keepdims=True)
    skip_ref[...] = jnp.broadcast_to(jnp.where(iota((1, 128), 1) < H, skip, 0.0), (8, 128))
    tokt_ref[...] = tok_ref[...].T


def gradient_kernel(
    core_ref, mine_ref, got_ref, xw_ref, ge_ref, x_ref, g_ref, bc_ref, proj_ref, tokt_ref,
    log_ref, dt_ref, sig_ref, rate_ref, direct_ref, du_ref, sgin_ref, cross_ref, col_ref, skip_ref,
    scan_ref, logit_ref, mixer_ref, keep_ref, send_ref,
    s_all, e_all, weight,
):
    spread = head_rows(N)
    core = core_ref[0]
    own = pl.multiple_of(core * HALF, HALF)
    other = pl.multiple_of(HALF - core * HALF, HALF)
    s_all[pl.ds(own, HALF), :] = mine_ref[0:HALF, :].astype(bf16)
    s_all[pl.ds(other, HALF), :] = got_ref[0:HALF, :].astype(bf16)
    e_all[pl.ds(own, HALF), :] = mine_ref[HALF:N, :].astype(bf16)
    e_all[pl.ds(other, HALF), :] = got_ref[HALF:N, :].astype(bf16)
    b = bc_ref[:, :N]
    c = bc_ref[:, N:]
    xw = xw_ref[...]
    ge = ge_ref[...]
    sg_b = sgin_ref[:, :N] + dot11(xw, e_all[...])
    sg_c = sgin_ref[:, N:] + dot11(ge, s_all[...])
    sg = jnp.concatenate([sg_b, sg_c], axis=1).astype(bf16)
    weight[...] = dot10(tokt_ref[...], sg)
    mixer_ref[...] = dot11(sg, proj_ref[...]).astype(bf16)
    log_decay = log_ref[...]
    dt = dt_ref[...]
    last = log_decay[:, T - 1 : T]
    to_end = widen(jnp.exp(last - log_decay) * dt, spread)
    eb = dot10(b, e_all[...])
    direct_row = jnp.broadcast_to(
        jnp.concatenate([direct_ref[...], jnp.zeros((1, 128 - H), f32)], axis=1), (8, 128)
    )
    direct = widen_row(direct_row, spread)[0:1]
    scan_ref[...] = (du_ref[...] + to_end * eb + direct * g_ref[...].astype(f32)).astype(bf16)
    pick = spread[0:48]
    v = dot11(pick, (xw.astype(f32) * eb).astype(bf16))[0:H]
    from_start = dot10(c, s_all[...])
    carry = dot11(pick, (ge.astype(f32) * from_start).astype(bf16))[0:H]
    meet = mine_ref[0:HALF, :] * mine_ref[HALF:N, :] + got_ref[0:HALF, :] * got_ref[HALF:N, :]
    meet = jnp.sum(meet.reshape(HALF // 8, 8, W), axis=0)
    meet = dot11(pick, jnp.concatenate(split3(meet), axis=0).astype(bf16))[0:H]
    through = jnp.sum(meet, axis=1, keepdims=True) * jnp.exp(last)
    row = iota((T, T), 0)
    col = iota((T, T), 1)
    log_grad = (
        through
        + over_positions(carry + cross_ref[...], row >= col)
        + over_positions(v, row < col)
    )
    rate = jnp.exp(column(rate_ref[...], H))
    dt_grad = (col_ref[...] + v) / dt - rate * log_grad
    logit = dt_grad * sig_ref[...]
    logit_ref[...] = logit
    on_lane = iota((H, 128), 0) == iota((H, 128), 1)

    def as_row(colsum):
        return jnp.sum(jnp.where(on_lane, colsum, 0.0), axis=0, keepdims=True)

    rate_row = as_row(jnp.sum(-rate * dt * log_grad, axis=1, keepdims=True))
    bias_row = as_row(jnp.sum(logit, axis=1, keepdims=True))
    params = jnp.concatenate(
        [
            jnp.concatenate([rate_row, bias_row], axis=1),
            jnp.concatenate([skip_ref[0:1, :], jnp.zeros((1, 128), f32)], axis=1),
            jnp.zeros((6, 256), f32),
        ],
        axis=0,
    )
    for chip in range(CHIPS):
        mine = pl.multiple_of((2 * chip + core) * ROWS, 8)
        theirs = pl.multiple_of((2 * chip + 1 - core) * ROWS, 8)
        keep_ref[chip, 0:ROWS, :] = weight[pl.ds(mine, ROWS), :]
        send_ref[chip, 0:ROWS, :] = weight[pl.ds(theirs, ROWS), :]
        keep_ref[chip, ROWS:PROWS, :] = params
        send_ref[chip, ROWS:PROWS, :] = params


def call(kernel, outs, scratch=(), smem=1, flops=0, moved=0, n_in=0):
    vmem = pl.BlockSpec(memory_space=pltpu.VMEM)
    return pl.pallas_call(
        kernel,
        out_shape=[jax.ShapeDtypeStruct(s, d) for s, d in outs],
        in_specs=[pl.BlockSpec(memory_space=pltpu.SMEM)] * smem + [vmem] * n_in,
        out_specs=[vmem] * len(outs),
        scratch_shapes=list(scratch),
        compiler_params=pltpu.CompilerParams(vmem_limit_bytes=48 * 1024 * 1024),
        cost_estimate=pl.CostEstimate(flops=flops, bytes_accessed=moved, transcendentals=0),
    )


def on_device(tokens, scan_input, logits, grads, proj, bias, rate_log, direct):
    tok, x, lg, g = tokens[0], scan_input[0], logits[0], grads[0]
    place = lax.axis_index("seq")
    core = lax.rem(place, 2).astype(jnp.int32).reshape(1)
    chip = lax.div(place, 2)
    back = (chip >= CHIPS // 2).astype(jnp.int32).reshape(1)
    bias_row = bias.reshape(1, H)
    rate_row = rate_log.reshape(1, H)
    direct_row = direct.reshape(1, H)
    swap = [(i, i ^ 1) for i in range(2 * CHIPS)]
    same_core = [[2 * i + k for i in range(CHIPS)] for k in range(2)]
    exchange = partial(
        lax.all_to_all, axis_name="seq", split_axis=0, concat_axis=0, axis_index_groups=same_core
    )

    bc, xw, ge, keep, send, log_decay, dt, sig = call(
        summary_kernel,
        [
            ((T, 2 * N), bf16), ((T, W), bf16), ((T, W), bf16),
            ((N, W + TAIL), f32), ((N, W + TAIL), f32),
            ((H, T), f32), ((H, T), f32), ((H, T), f32),
        ],
        [pltpu.VMEM((2 * N, W), f32)],
        n_in=7, flops=int(1e9), moved=int(1e7),
    )(core, tok, x, g, proj, lg, bias_row, rate_row)
    got = lax.ppermute(send, "seq", swap)
    (chips,) = call(
        chip_kernel, [((N, W + TAIL), f32)], n_in=2, flops=int(1e7), moved=int(4e6)
    )(core, keep, got)
    owned = exchange(chips.reshape(CHIPS, 8, W + TAIL))
    du, sg_in, cross, col, skip, tokt = call(
        within_kernel,
        [
            ((T, W), f32), ((T, 2 * N), f32), ((H, T), f32), ((H, T), f32), ((8, 128), f32),
            ((W, T), bf16),
        ],
        [
            pltpu.VMEM((T, W), f32), pltpu.VMEM((H, T), f32),
            pltpu.VMEM((T, T), f32), pltpu.VMEM((T, 128), f32),
        ],
        smem=0, n_in=6, flops=int(8e9), moved=int(1e7),
    )(tok, x, g, bc, log_decay, dt)
    (starts,) = call(
        scan_kernel, [((CHIPS, 8, W), f32)], [pltpu.VMEM((CHIPS, 8, W), f32)], n_in=2,
        flops=int(1e7), moved=int(3e6),
    )(back, owned, skip)
    returned = exchange(starts).reshape(N, W)
    mine, send2 = call(
        core_kernel, [((N, W), f32), ((N, W), f32)], n_in=3, flops=int(1e7), moved=int(6e6)
    )(core, returned, keep, got)
    got2 = lax.ppermute(send2, "seq", swap)
    scan_grad, logit_grad, mixer_grad, wkeep, wsend = call(
        gradient_kernel,
        [
            ((T, W), bf16), ((H, T), f32), ((T, W), bf16),
            ((CHIPS, PROWS, 2 * N), f32), ((CHIPS, PROWS, 2 * N), f32),
        ],
        [pltpu.VMEM((N, W), bf16), pltpu.VMEM((N, W), bf16), pltpu.VMEM((W, 2 * N), f32)],
        n_in=19, flops=int(3e9), moved=int(2e7),
    )(
        core, mine, got2, xw, ge, x, g, bc, proj, tokt, log_decay, dt, sig, rate_row, direct_row,
        du, sg_in, cross, col, skip,
    )
    wsum = wkeep + lax.ppermute(wsend, "seq", swap)
    total = jnp.sum(exchange(wsum), axis=0)
    for k in (1, 2, 4):
        total = total + lax.ppermute(total, "dp", [(i, i ^ k) for i in range(8)])
    total = total * (float(T * 2 * CHIPS * 8) ** -0.5)
    return (
        scan_grad[None],
        logit_grad[None],
        mixer_grad[None],
        total[0:ROWS],
        total[ROWS, 0:H],
        total[ROWS + 1, 0:H],
        total[ROWS, N : N + H],
    )


def solution(mesh):
    placed = (
        P("dp", "seq", None),
        P("dp", "seq", None),
        P("dp", None, "seq"),
        P("dp", "seq", None),
        P(),
        P(),
        P(),
        P(),
    )
    return jax.shard_map(
        on_device,
        mesh=mesh,
        in_specs=placed,
        out_specs=(
            P("dp", "seq", None),
            P("dp", None, "seq"),
            P("dp", "seq", None),
            P("seq", None),
            P(),
            P(),
            P(),
        ),
        check_vma=False,
    )
```

```python
from functools import partial

import jax
import jax.numpy as jnp
from jax import lax
from jax.sharding import PartitionSpec as P
import jax.experimental.pallas as pl
import jax.experimental.pallas.tpu as pltpu

f32 = jnp.float32
bf16 = jnp.bfloat16

T = 256
H = 40
HD = 64
W = 2560
N = 128
HALF = 64
TAIL = 128
CHIPS = 16
ROWS = 80
PROWS = 88


def iota(shape, dim):
    return lax.broadcasted_iota(jnp.int32, shape, dim)


def split3(v):
    hi = v.astype(bf16).astype(f32)
    rest = v - hi
    mid = rest.astype(bf16).astype(f32)
    return hi, mid, rest - mid


def dot00(a, b):
    return lax.dot_general(a, b, (((0,), (0,)), ((), ())), preferred_element_type=f32)


def dot11(a, b):
    return lax.dot_general(a, b, (((1,), (1,)), ((), ())), preferred_element_type=f32)


def dot10(a, b):
    return lax.dot_general(a, b, (((1,), (0,)), ((), ())), preferred_element_type=f32)


def head_rows(count):
    lane_head = iota((count, W), 1) >> 6
    row = iota((count, W), 0)
    hit = (lane_head == row) | (lane_head == row - H) | (lane_head == row - 2 * H)
    return jnp.where(hit, 1.0, 0.0).astype(bf16)


def widen(v, spread):
    parts = jnp.concatenate(split3(v) + (jnp.zeros((8, T), f32),), axis=0).astype(bf16)
    return dot00(parts, spread)


def widen_row(row, spread):
    parts = jnp.concatenate(split3(row) + (jnp.zeros((8, 128), f32),), axis=0).astype(bf16)
    lanes = iota((N, W), 0) < H
    once = jnp.where(lanes, spread.astype(f32), 0.0).astype(bf16)
    out = dot10(parts, once)
    return out[0:8] + out[8:16] + out[16:24]


def column(row, count):
    eye = iota((count, count), 0) == iota((count, count), 1)
    return jnp.sum(jnp.where(eye, row, 0.0), axis=1, keepdims=True)


def over_positions(v, keep):
    parts = jnp.concatenate(split3(v) + (jnp.zeros((8, T), f32),), axis=0).astype(bf16)
    out = dot10(parts, jnp.where(keep, 1.0, 0.0).astype(bf16))
    return out[0:H] + out[H : 2 * H] + out[2 * H : 3 * H]


def step_sizes(logits, bias_row):
    z = logits + column(bias_row, H)
    e = jnp.exp(-jnp.abs(z))
    r = e / (2.0 + e)
    r2 = r * r
    poly = 1.0 / 17.0
    for odd in (15, 13, 11, 9, 7, 5, 3):
        poly = poly * r2 + 1.0 / odd
    dt = jnp.maximum(z, 0.0) + 2.0 * (r + r * r2 * poly)
    sig = jnp.where(z >= 0.0, 1.0, e) / (1.0 + e)
    return dt, sig


def summary_kernel(
    core_ref, bias_ref, rate_ref, logit_hbm, tok_hbm, x_hbm, g_hbm, proj_hbm,
    bc_ref, xw_ref, ge_ref, keep_ref, send_ref, more_ref, log_ref, dt_ref,
    logit_ref, tok_ref, x_ref, g_ref, proj_ref, both, sem,
):
    pairs = (
        (logit_hbm, logit_ref), (tok_hbm, tok_ref), (proj_hbm, proj_ref), (x_hbm, x_ref), (g_hbm, g_ref)
    )
    copies = [pltpu.make_async_copy(a, b, sem.at[i]) for i, (a, b) in enumerate(pairs)]
    for copy in copies:
        copy.start()
    spread = head_rows(N)
    copies[0].wait()
    dt, _ = step_sizes(logit_ref[...], bias_ref[...])
    rate = jnp.exp(column(rate_ref[...], H))
    log_decay = over_positions(-rate * dt, iota((T, T), 0) <= iota((T, T), 1))
    last = log_decay[:, T - 1 : T]
    log_ref[...] = log_decay
    dt_ref[...] = dt
    copies[1].wait()
    copies[2].wait()
    bc = dot10(tok_ref[...], proj_ref[...]).astype(bf16)
    bc_ref[...] = bc
    copies[3].wait()
    copies[4].wait()
    xw = (x_ref[...].astype(f32) * widen(jnp.exp(last - log_decay) * dt, spread)).astype(bf16)
    xw_ref[...] = xw
    ge = (g_ref[...].astype(f32) * widen(jnp.exp(log_decay), spread)).astype(bf16)
    ge_ref[...] = ge
    both[0:N, :] = dot00(bc[:, :N], xw)
    both[N : 2 * N, :] = dot00(bc[:, N:], ge)
    mine = pl.multiple_of(core_ref[0] * HALF, HALF)
    theirs = pl.multiple_of(HALF - core_ref[0] * HALF, HALF)
    keep_ref[0:HALF, 0:W] = both[pl.ds(mine, HALF), :]
    keep_ref[HALF:N, 0:W] = both[pl.ds(N + mine, HALF), :]
    send_ref[0:HALF, 0:W] = both[pl.ds(theirs, HALF), :]
    send_ref[HALF:N, 0:W] = both[pl.ds(N + theirs, HALF), :]
    more_ref[...] = both[pl.ds(pl.multiple_of(core_ref[0] * (N + HALF), HALF), HALF), :]
    on_lane = iota((H, TAIL), 0) == iota((H, TAIL), 1)
    decay = jnp.exp(jnp.sum(jnp.where(on_lane, last, 0.0), axis=0, keepdims=True))
    decay = jnp.broadcast_to(decay, (N, TAIL))
    keep_ref[:, W:] = decay
    send_ref[:, W:] = decay


def chip_kernel(core_ref, keep_ref, got_ref, out_ref):
    spread = head_rows(N)
    decay_mine = keep_ref[0:8, W:]
    decay_their = got_ref[0:8, W:]
    wide_mine = widen_row(decay_mine, spread)[0:1]
    wide_their = widen_row(decay_their, spread)[0:1]
    first = core_ref[0] == 0
    one = jnp.ones((1, W), f32)
    a = jnp.where(first, wide_their, one)
    b = jnp.where(first, one, wide_mine)
    c = jnp.where(first, one, wide_their)
    d = jnp.where(first, wide_mine, one)
    out_ref[0:HALF, 0:W] = a * keep_ref[0:HALF, 0:W] + b * got_ref[0:HALF, 0:W]
    out_ref[HALF:N, 0:W] = c * keep_ref[HALF:N, 0:W] + d * got_ref[HALF:N, 0:W]
    out_ref[:, W:] = keep_ref[:, W:] * got_ref[:, W:]


def scan_kernel(back_ref, in_ref, after_ref, out_ref, wide):
    spread = head_rows(N)
    for c in range(CHIPS):
        wide[c] = widen_row(in_ref[c, :, W:], spread)
    back = back_ref[0]
    state = jnp.zeros((8, W), f32)
    for i in range(CHIPS):
        c = jnp.where(back == 1, CHIPS - 1 - i, i)
        out_ref[c] = state
        state = wide[c] * state + in_ref[c, :, 0:W]


def within_kernel(
    first, x_ref, g_ref, bc_ref, log_ref, dt_ref, before_ref,
    du_ref, sg_ref, cross_ref, col_ref,
    wide_log, late_log, ds, rows,
):
    half = T // 2
    spread = head_rows(N)
    log_decay = log_ref[...]
    dt = dt_ref[...]
    wide_log[...] = widen(log_decay, spread)
    late_log[...] = log_decay - jnp.log(dt)
    b = bc_ref[:, :N]
    c = bc_ref[:, N:]
    scores = dot11(c, b)
    ds[...] = jnp.zeros((T, T), f32)
    rows[...] = jnp.zeros((T, 128), f32)
    col_ref[...] = jnp.zeros((H, T), f32)
    causal = iota((half, half), 0) >= iota((half, half), 1)
    lane = iota((T, 128), 1)

    def pair(i, carry):
        cols = pl.ds(pl.multiple_of((first + i) * 128, 128), 128)
        xp = x_ref[:, cols]
        gp = g_ref[:, cols]
        logs = wide_log[:, cols]
        total = jnp.zeros((T, 128), f32)
        for m in range(2):
            h = 2 * (first + i) + m
            gm = jnp.where((lane >= HD) == (m == 1), gp.astype(f32), 0.0).astype(bf16)
            q0 = dot11(gm[0:half], xp[0:half])
            q1 = dot11(gm[half:], xp)
            late = late_log[pl.ds(h, 1), :]
            lc = logs[:, m * HD : m * HD + 1]
            gap0 = lc[0:half] - late[:, 0:half]
            gap1 = lc[half:] - late[:, half:]
            dec0 = jnp.exp(jnp.where(causal, gap0, -1e30))
            dec1 = jnp.concatenate(
                [
                    jnp.exp(lc[half:] - late[:, 0:half]),
                    jnp.exp(jnp.where(causal, gap1, -1e30)),
                ],
                axis=1,
            )
            m0 = dec0 * scores[0:half, 0:half]
            m1 = dec1 * scores[half:, :]
            ds[0:half, 0:half] += dec0 * q0
            ds[half:, :] += dec1 * q1
            p0 = m0 * q0
            p1 = m1 * q1
            rsum = jnp.concatenate(
                [jnp.sum(p0, axis=1, keepdims=True), jnp.sum(p1, axis=1, keepdims=True)], axis=0
            )
            rows[...] += jnp.where(lane == h, rsum, 0.0)
            csum1 = jnp.sum(p1, axis=0, keepdims=True)
            csum0 = jnp.sum(p0, axis=0, keepdims=True)
            col_ref[pl.ds(h, 1), :] = csum1 + jnp.concatenate(
                [csum0, jnp.zeros((1, half), f32)], axis=1
            )
            early = dot00(m0.astype(bf16), gm[0:half])
            late_part = dot00(m1.astype(bf16), gm[half:])
            total = total + late_part + jnp.concatenate(
                [early, jnp.zeros((half, 128), f32)], axis=0
            )
        du_ref[:, pl.ds(pl.multiple_of(i * 128, 128), 128)] = total
        return carry

    lax.fori_loop(0, H // 4, pair, 0)
    hi, mid, _ = split3(ds[...])
    hi = hi.astype(bf16)
    mid = mid.astype(bf16)
    sg_ref[:, :N] = before_ref[:, :N] + dot00(hi, c) + dot00(mid, c)
    sg_ref[:, N:] = before_ref[:, N:] + dot10(hi, b) + dot10(mid, b)
    cross_ref[...] = rows[...].T[0:H, :] - col_ref[...]


def token_kernel(
    core_ref, tok_ref, x_ref, g_ref, logit_ref, bias_ref,
    keep_ref, send_ref, sig_ref, skip_ref, turned,
):
    spread = head_rows(N)
    turned[...] = tok_ref[...].T
    for chip in range(CHIPS):
        mine = pl.multiple_of((2 * chip + core_ref[0]) * ROWS, 16)
        theirs = pl.multiple_of((2 * chip + 1 - core_ref[0]) * ROWS, 16)
        keep_ref[chip * ROWS : (chip + 1) * ROWS, :] = turned[pl.ds(mine, ROWS), :]
        send_ref[chip * ROWS : (chip + 1) * ROWS, :] = turned[pl.ds(theirs, ROWS), :].astype(f32)
    x = x_ref[...].astype(f32)
    g = g_ref[...].astype(f32)
    _, sig_ref[...] = step_sizes(logit_ref[...], bias_ref[...])
    part = jnp.sum((x * g).reshape(T // 8, 8, W), axis=0)
    skip = dot11(jnp.concatenate(split3(part), axis=0).astype(bf16), spread)
    skip = jnp.sum(skip, axis=0, keepdims=True)
    skip_ref[...] = jnp.broadcast_to(jnp.where(iota((1, 128), 1) < H, skip, 0.0), (8, 128))


def half_states(first, decay, chip_ref, extra):
    one = jnp.ones((1, W), f32)
    zero = jnp.zeros((1, W), f32)
    s = jnp.where(first, one, decay) * chip_ref[0:HALF, :] + jnp.where(first, zero, one) * extra
    e = jnp.where(first, decay, one) * chip_ref[HALF:N, :] + jnp.where(first, one, zero) * extra
    return s, e, jnp.sum((s * e).reshape(HALF // 8, 8, W), axis=0)


def near_kernel(core_ref, chip_ref, got_ref, xw_ref, ge_ref, s_ref, e_ref, meet_ref, part_ref, decay_ref):
    first = core_ref[0] == 0
    wide = widen_row(got_ref[0:8, W:], head_rows(N))[0:1]
    extra = jnp.where(first, got_ref[HALF:N, 0:W], got_ref[0:HALF, 0:W])
    decay_ref[...] = got_ref[0:8, W:]
    s, e, meet_ref[...] = half_states(first, wide, chip_ref, extra)
    s_ref[...] = s.astype(bf16)
    e_ref[...] = e.astype(bf16)
    part_ref[...] = jnp.concatenate(
        [dot11(xw_ref[...], e_ref[...]), dot11(ge_ref[...], s_ref[...])], axis=1
    )


def state_kernel(
    core_ref, chip_ref, more_ref, near_s_ref, near_e_ref, near_meet_ref, part_ref, decay_ref,
    xw_ref, ge_ref, sgin_ref,
    sg_ref, sgsend_ref, s_ref, e_ref, meet_ref,
):
    core = core_ref[0]
    first = core == 0
    wide = widen_row(decay_ref[...], head_rows(N))[0:1]
    s, e, meet = half_states(first, wide, chip_ref, more_ref[...])
    meet_ref[...] = near_meet_ref[...] + meet
    s = s.astype(bf16)
    e = e.astype(bf16)
    own = pl.ds(pl.multiple_of(core * HALF, HALF), HALF)
    other = pl.ds(pl.multiple_of(HALF - core * HALF, HALF), HALF)
    s_ref[own, :] = near_s_ref[...]
    e_ref[own, :] = near_e_ref[...]
    s_ref[other, :] = s
    e_ref[other, :] = e
    far = jnp.concatenate([dot11(xw_ref[...], e), dot11(ge_ref[...], s)], axis=1)
    near = part_ref[...]
    lo = jnp.where(first, near, far)
    hi = jnp.where(first, far, near)
    sg = sgin_ref[...] + jnp.concatenate(
        [lo[:, :HALF], hi[:, :HALF], lo[:, HALF:], hi[:, HALF:]], axis=1
    )
    sg = sg.astype(bf16)
    sg_ref[...] = sg
    sgsend_ref[...] = sg.astype(f32)


def own_weight_kernel(keep_ref, sg_ref, out_ref):
    out_ref[...] = dot10(keep_ref[...], sg_ref[...])


def weight_kernel(own_ref, got_ref, sggot_ref, param_ref, paramgot_ref, out_ref):
    out = own_ref[...] + dot10(got_ref[...].astype(bf16), sggot_ref[...].astype(bf16))
    out_ref[:, 0:ROWS, :] = out.reshape(CHIPS, ROWS, 2 * N)
    params = param_ref[...] + paramgot_ref[...]
    params = jnp.concatenate([params, jnp.zeros_like(params)], axis=1)
    out_ref[:, ROWS:PROWS, :] = jnp.broadcast_to(params[None], (CHIPS, 8, 2 * N))


def logit_kernel(
    s_ref, e_ref, meet_ref, xw_ref, ge_ref, bc_ref, log_ref, dt_ref, sig_ref, rate_ref,
    crossa_ref, crossb_ref, cola_ref, colb_ref, skip_ref,
    logit_ref, param_ref,
):
    spread = head_rows(N)
    b = bc_ref[:, :N]
    c = bc_ref[:, N:]
    log_decay = log_ref[...]
    dt = dt_ref[...]
    last = log_decay[:, T - 1 : T]
    pick = spread[0:48]
    eb = dot10(b, e_ref[...])
    v = dot11(pick, (xw_ref[...].astype(f32) * eb).astype(bf16))[0:H]
    from_start = dot10(c, s_ref[...])
    carry = dot11(pick, (ge_ref[...].astype(f32) * from_start).astype(bf16))[0:H]
    meet = dot11(pick, jnp.concatenate(split3(meet_ref[...]), axis=0).astype(bf16))[0:H]
    through = jnp.sum(meet, axis=1, keepdims=True) * jnp.exp(last)
    row = iota((T, T), 0)
    col = iota((T, T), 1)
    log_grad = (
        through
        + over_positions(carry + crossa_ref[...] + crossb_ref[...], row >= col)
        + over_positions(v, row < col)
    )
    rate = jnp.exp(column(rate_ref[...], H))
    dt_grad = (cola_ref[...] + colb_ref[...] + v) / dt - rate * log_grad
    logit = dt_grad * sig_ref[...]
    logit_ref[...] = logit
    on_lane = iota((H, 128), 0) == iota((H, 128), 1)

    def as_row(colsum):
        return jnp.sum(jnp.where(on_lane, colsum, 0.0), axis=0, keepdims=True)

    rate_row = as_row(jnp.sum(-rate * dt * log_grad, axis=1, keepdims=True))
    bias_row = as_row(jnp.sum(logit, axis=1, keepdims=True))
    param_ref[...] = jnp.concatenate(
        [rate_row, bias_row, skip_ref[0:1, :], jnp.zeros((5, 128), f32)], axis=0
    )


def scan_grad_kernel(
    e_ref, g_ref, bc_ref, log_ref, dt_ref, direct_ref, dua_ref, dub_ref, scan_ref
):
    spread = head_rows(N)
    log_decay = log_ref[...]
    eb = dot10(bc_ref[:, :N], e_ref[...])
    to_end = widen(jnp.exp(log_decay[:, T - 1 : T] - log_decay) * dt_ref[...], spread)
    direct_row = jnp.broadcast_to(
        jnp.concatenate([direct_ref[...], jnp.zeros((1, 128 - H), f32)], axis=1), (8, 128)
    )
    direct = widen_row(direct_row, spread)[0:1]
    half = W // 2
    for at, ref in ((0, dua_ref), (half, dub_ref)):
        to = slice(at, at + half)
        scan_ref[:, to] = (
            ref[...] + to_end[:, to] * eb[:, to] + direct[:, to] * g_ref[:, to].astype(f32)
        ).astype(bf16)


def mixer_kernel(sg_ref, proj_ref, mixer_ref):
    mixer_ref[...] = dot11(sg_ref[...], proj_ref[...]).astype(bf16)


def call(kernel, outs, scratch=(), smem=1, far=0, flops=0, moved=0, n_in=0, mib=32):
    vmem = pl.BlockSpec(memory_space=pltpu.VMEM)
    return pl.pallas_call(
        kernel,
        out_shape=[jax.ShapeDtypeStruct(s, d) for s, d in outs],
        in_specs=[pl.BlockSpec(memory_space=pltpu.SMEM)] * smem
        + [vmem] * n_in
        + [pl.BlockSpec(memory_space=pltpu.HBM)] * far,
        out_specs=[vmem] * len(outs),
        scratch_shapes=list(scratch),
        compiler_params=pltpu.CompilerParams(vmem_limit_bytes=mib * 1024 * 1024),
        cost_estimate=pl.CostEstimate(flops=flops, bytes_accessed=moved, transcendentals=0),
    )


def on_device(tokens, scan_input, logits, grads, proj, bias, rate_log, direct):
    tok, x, lg, g = tokens[0], scan_input[0], logits[0], grads[0]
    place = lax.axis_index("seq")
    core = lax.rem(place, 2).astype(jnp.int32).reshape(1)
    chip = lax.div(place, 2)
    back = (chip >= CHIPS // 2).astype(jnp.int32).reshape(1)
    bias_row = bias.reshape(1, H)
    rate_row = rate_log.reshape(1, H)
    direct_row = direct.reshape(1, H)
    swap = [(i, i ^ 1) for i in range(2 * CHIPS)]
    same_core = [[2 * i + k for i in range(CHIPS)] for k in range(2)]
    exchange = partial(
        lax.all_to_all, axis_name="seq", split_axis=0, concat_axis=0, axis_index_groups=same_core
    )

    bc, xw, ge, keep, send, more, log_decay, dt = call(
        summary_kernel,
        [
            ((T, 2 * N), bf16), ((T, W), bf16), ((T, W), bf16),
            ((N, W + TAIL), f32), ((N, W + TAIL), f32), ((HALF, W), f32),
            ((H, T), f32), ((H, T), f32),
        ],
        [
            pltpu.VMEM((H, T), f32), pltpu.VMEM((T, W), bf16), pltpu.VMEM((T, W), bf16),
            pltpu.VMEM((T, W), bf16), pltpu.VMEM((W, 2 * N), bf16), pltpu.VMEM((2 * N, W), f32),
            pltpu.SemaphoreType.DMA((5,)),
        ],
        n_in=2, far=5, flops=int(1e9), moved=int(1e7), mib=50,
    )(core, bias_row, rate_row, lg, tok, x, g, proj)
    got = lax.ppermute(send, "seq", swap)
    (chips,) = call(
        chip_kernel, [((N, W + TAIL), f32)], n_in=2, flops=int(1e7), moved=int(4e6), mib=8
    )(core, keep, got)
    chips, tok_b = lax.optimization_barrier((chips, tok))
    owned = exchange(chips.reshape(CHIPS, 8, W + TAIL))

    def within(first, dt, before):
        return call(
            partial(within_kernel, first),
            [((T, W // 2), f32), ((T, 2 * N), f32), ((H, T), f32), ((H, T), f32)],
            [
                pltpu.VMEM((T, W), f32), pltpu.VMEM((H, T), f32),
                pltpu.VMEM((T, T), f32), pltpu.VMEM((T, 128), f32),
            ],
            smem=0, n_in=6, flops=int(8e9), moved=int(5e6), mib=56,
        )(x, g, bc, log_decay, dt, before)

    du_a, sg_a, cross_a, col_a = within(0, dt, jnp.zeros((T, 2 * N), f32))
    tokt, tokt_send, sig, skip = call(
        token_kernel,
        [
            ((W // 2, T), bf16), ((W // 2, T), f32), ((H, T), f32), ((8, 128), f32),
        ],
        [pltpu.VMEM((W, T), bf16)],
        n_in=5, flops=int(3e9), moved=int(8e6), mib=56,
    )(core, tok_b, x, g, lg, bias_row)
    tokt_got = lax.ppermute(tokt_send, "seq", swap)
    more = lax.ppermute(more, "seq", swap)
    (starts,) = call(
        scan_kernel, [((CHIPS, 8, W), f32)], [pltpu.VMEM((CHIPS, 8, W), f32)],
        n_in=2, flops=int(1e7), moved=int(3e6), mib=6,
    )(back, owned, col_a)
    returned = exchange(starts).reshape(N, W)
    _, more, tokt_got, dt_b = lax.optimization_barrier((starts, more, tokt_got, dt))
    du_b, sg_b, cross_b, col_b = within(H // 4, dt_b, sg_a)
    returned, sg_b = lax.optimization_barrier((returned, sg_b))
    returned_got = lax.ppermute(returned, "seq", swap)
    near_s, near_e, near_meet, near_part, decay = call(
        near_kernel,
        [((HALF, W), bf16), ((HALF, W), bf16), ((8, W), f32), ((T, N), f32), ((8, TAIL), f32)],
        n_in=4, flops=int(4e8), moved=int(6e6), mib=10,
    )(core, returned, got, xw, ge)
    sg, sg_send, s_all, e_all, meet = call(
        state_kernel,
        [
            ((T, 2 * N), bf16), ((T, 2 * N), f32), ((N, W), bf16), ((N, W), bf16), ((8, W), f32)
        ],
        n_in=10, flops=int(4e8), moved=int(6e6), mib=10,
    )(
        core, returned_got, more, near_s, near_e, near_meet, near_part, decay, xw, ge, sg_b
    )
    sg_got = lax.ppermute(sg_send, "seq", swap)
    logit_grad, params = call(
        logit_kernel, [((H, T), f32), ((8, 128), f32)], smem=0, n_in=15,
        flops=int(4e8), moved=int(4e6), mib=10,
    )(
        s_all, e_all, meet, xw, ge, bc, log_decay, dt, sig, rate_row,
        cross_a, cross_b, col_a, col_b, skip,
    )
    params_got = lax.ppermute(params, "seq", swap)
    (own_weights,) = call(
        own_weight_kernel, [((W // 2, 2 * N), f32)], smem=0, n_in=2,
        flops=int(2e8), moved=int(2e6), mib=6,
    )(tokt, sg)
    (weights,) = call(
        weight_kernel, [((CHIPS, PROWS, 2 * N), f32)], smem=0, n_in=5,
        flops=int(2e8), moved=int(4e6), mib=8,
    )(own_weights, tokt_got, sg_got, params, params_got)
    parts = exchange(weights)
    parts, e_late, sg_late = lax.optimization_barrier((parts, e_all, sg))
    (scan_grad,) = call(
        scan_grad_kernel, [((T, W), bf16)], smem=0, n_in=8, flops=int(2e9), moved=int(1e7), mib=56,
    )(e_late, g, bc, log_decay, dt, direct_row, du_a, du_b)
    (mixer_grad,) = call(
        mixer_kernel, [((T, W), bf16)], smem=0, n_in=2, flops=int(1e9), moved=int(3e6), mib=56,
    )(sg_late, proj)
    total = jnp.sum(parts, axis=0)
    for k in (1, 2, 4):
        total = total + lax.ppermute(total, "dp", [(i, i ^ k) for i in range(8)])
    total = total * (float(T * 2 * CHIPS * 8) ** -0.5)
    return (
        scan_grad[None],
        logit_grad[None],
        mixer_grad[None],
        total[0:ROWS],
        total[ROWS, 0:H],
        total[ROWS + 2, 0:H],
        total[ROWS + 1, 0:H],
    )


def solution(mesh):
    placed = (
        P("dp", "seq", None),
        P("dp", "seq", None),
        P("dp", None, "seq"),
        P("dp", "seq", None),
        P(),
        P(),
        P(),
        P(),
    )
    return jax.shard_map(
        on_device,
        mesh=mesh,
        in_specs=placed,
        out_specs=(
            P("dp", "seq", None),
            P("dp", None, "seq"),
            P("dp", "seq", None),
            P("seq", None),
            P(),
            P(),
            P(),
        ),
        check_vma=False,
    )
```

```python
from functools import partial

import jax
import jax.numpy as jnp
from jax import lax
from jax.sharding import PartitionSpec as P
import jax.experimental.pallas as pl
import jax.experimental.pallas.tpu as pltpu

f32 = jnp.float32
bf16 = jnp.bfloat16

T = 256
H = 40
HD = 64
W = 2560
N = 128
HALF = 64
TAIL = 128
CHIPS = 16
ROWS = 80
PROWS = 88


def iota(shape, dim):
    return lax.broadcasted_iota(jnp.int32, shape, dim)


def split3(v):
    hi = v.astype(bf16).astype(f32)
    rest = v - hi
    mid = rest.astype(bf16).astype(f32)
    return hi, mid, rest - mid


def dot00(a, b):
    return lax.dot_general(a, b, (((0,), (0,)), ((), ())), preferred_element_type=f32)


def dot11(a, b):
    return lax.dot_general(a, b, (((1,), (1,)), ((), ())), preferred_element_type=f32)


def dot10(a, b):
    return lax.dot_general(a, b, (((1,), (0,)), ((), ())), preferred_element_type=f32)


def head_rows(count, first=0, width=W):
    lane_head = (iota((count, width), 1) + first) >> 6
    row = iota((count, width), 0)
    hit = (lane_head == row) | (lane_head == row - H) | (lane_head == row - 2 * H)
    return jnp.where(hit, 1.0, 0.0).astype(bf16)


def widen(v, spread):
    parts = jnp.concatenate(split3(v) + (jnp.zeros((8, T), f32),), axis=0).astype(bf16)
    return dot00(parts, spread)


def widen_row(row, spread):
    parts = jnp.concatenate(split3(row) + (jnp.zeros((8, 128), f32),), axis=0).astype(bf16)
    lanes = iota(spread.shape, 0) < H
    once = jnp.where(lanes, spread.astype(f32), 0.0).astype(bf16)
    out = dot10(parts, once)
    return out[0:8] + out[8:16] + out[16:24]


def column(row, count):
    eye = iota((count, count), 0) == iota((count, count), 1)
    return jnp.sum(jnp.where(eye, row, 0.0), axis=1, keepdims=True)


def over_positions(v, keep):
    parts = jnp.concatenate(split3(v) + (jnp.zeros((8, T), f32),), axis=0).astype(bf16)
    out = dot10(parts, jnp.where(keep, 1.0, 0.0).astype(bf16))
    return out[0:H] + out[H : 2 * H] + out[2 * H : 3 * H]


def step_sizes(logits, bias_row):
    z = logits + column(bias_row, H)
    e = jnp.exp(-jnp.abs(z))
    r = e / (2.0 + e)
    r2 = r * r
    poly = 1.0 / 17.0
    for odd in (15, 13, 11, 9, 7, 5, 3):
        poly = poly * r2 + 1.0 / odd
    dt = jnp.maximum(z, 0.0) + 2.0 * (r + r * r2 * poly)
    sig = jnp.where(z >= 0.0, 1.0, e) / (1.0 + e)
    return dt, sig


def summary_kernel(
    core_ref, bias_ref, rate_ref, logit_hbm, tok_hbm, x_hbm, g_hbm, proj_hbm,
    bc_ref, xw_ref, ge_ref, keep_ref, send_ref, more_ref, log_ref, dt_ref,
    logit_ref, tok_ref, x_ref, g_ref, proj_ref, both, sem,
):
    pairs = (
        (logit_hbm, logit_ref), (tok_hbm, tok_ref), (proj_hbm, proj_ref), (x_hbm, x_ref), (g_hbm, g_ref)
    )
    copies = [pltpu.make_async_copy(a, b, sem.at[i]) for i, (a, b) in enumerate(pairs)]
    for copy in copies:
        copy.start()
    spread = head_rows(N)
    copies[0].wait()
    dt, _ = step_sizes(logit_ref[...], bias_ref[...])
    rate = jnp.exp(column(rate_ref[...], H))
    log_decay = over_positions(-rate * dt, iota((T, T), 0) <= iota((T, T), 1))
    last = log_decay[:, T - 1 : T]
    log_ref[...] = log_decay
    dt_ref[...] = dt
    copies[1].wait()
    copies[2].wait()
    bc = dot10(tok_ref[...], proj_ref[...]).astype(bf16)
    bc_ref[...] = bc
    copies[3].wait()
    copies[4].wait()
    xw = (x_ref[...].astype(f32) * widen(jnp.exp(last - log_decay) * dt, spread)).astype(bf16)
    xw_ref[...] = xw
    ge = (g_ref[...].astype(f32) * widen(jnp.exp(log_decay), spread)).astype(bf16)
    ge_ref[...] = ge
    both[0:N, :] = dot00(bc[:, :N], xw)
    both[N : 2 * N, :] = dot00(bc[:, N:], ge)
    mine = pl.multiple_of(core_ref[0] * HALF, HALF)
    theirs = pl.multiple_of(HALF - core_ref[0] * HALF, HALF)
    keep_ref[0:HALF, 0:W] = both[pl.ds(mine, HALF), :]
    keep_ref[HALF:N, 0:W] = both[pl.ds(N + mine, HALF), :]
    send_ref[0:HALF, 0:W] = both[pl.ds(theirs, HALF), :]
    send_ref[HALF:N, 0:W] = both[pl.ds(N + theirs, HALF), :]
    more_ref[...] = both[pl.ds(pl.multiple_of(core_ref[0] * (N + HALF), HALF), HALF), :]
    on_lane = iota((H, TAIL), 0) == iota((H, TAIL), 1)
    decay = jnp.exp(jnp.sum(jnp.where(on_lane, last, 0.0), axis=0, keepdims=True))
    decay = jnp.broadcast_to(decay, (N, TAIL))
    keep_ref[:, W:] = decay
    send_ref[:, W:] = decay


def chip_kernel(core_ref, keep_ref, got_ref, out_ref):
    spread = head_rows(N)
    decay_mine = keep_ref[0:8, W:]
    decay_their = got_ref[0:8, W:]
    wide_mine = widen_row(decay_mine, spread)[0:1]
    wide_their = widen_row(decay_their, spread)[0:1]
    first = core_ref[0] == 0
    one = jnp.ones((1, W), f32)
    a = jnp.where(first, wide_their, one)
    b = jnp.where(first, one, wide_mine)
    c = jnp.where(first, one, wide_their)
    d = jnp.where(first, wide_mine, one)
    out_ref[0:HALF, 0:W] = a * keep_ref[0:HALF, 0:W] + b * got_ref[0:HALF, 0:W]
    out_ref[HALF:N, 0:W] = c * keep_ref[HALF:N, 0:W] + d * got_ref[HALF:N, 0:W]
    out_ref[:, W:] = keep_ref[:, W:] * got_ref[:, W:]


def scan_kernel(back_ref, in_ref, out_ref, wide):
    spread = head_rows(N)
    for c in range(CHIPS):
        wide[c] = widen_row(in_ref[c, :, W:], spread)
    back = back_ref[0]
    state = jnp.zeros((8, W), f32)
    for i in range(CHIPS):
        c = jnp.where(back == 1, CHIPS - 1 - i, i)
        out_ref[c] = state
        state = wide[c] * state + in_ref[c, :, 0:W]


def within_kernel(
    first, x_ref, g_ref, bc_ref, log_ref, dt_ref, before_ref,
    du_ref, sg_ref, cross_ref, col_ref,
    wide_log, late_log, ds, rows,
):
    half = T // 2
    spread = head_rows(N)
    log_decay = log_ref[...]
    dt = dt_ref[...]
    wide_log[...] = widen(log_decay, spread)
    late_log[...] = log_decay - jnp.log(dt)
    b = bc_ref[:, :N]
    c = bc_ref[:, N:]
    scores = dot11(c, b)
    ds[...] = jnp.zeros((T, T), f32)
    rows[...] = jnp.zeros((T, 128), f32)
    col_ref[...] = jnp.zeros((H, T), f32)
    causal = iota((half, half), 0) >= iota((half, half), 1)
    lane = iota((T, 128), 1)

    def pair(i, carry):
        cols = pl.ds(pl.multiple_of((first + i) * 128, 128), 128)
        xp = x_ref[:, cols]
        gp = g_ref[:, cols]
        logs = wide_log[:, cols]
        total = jnp.zeros((T, 128), f32)
        for m in range(2):
            h = 2 * (first + i) + m
            gm = jnp.where((lane >= HD) == (m == 1), gp.astype(f32), 0.0).astype(bf16)
            q0 = dot11(gm[0:half], xp[0:half])
            q1 = dot11(gm[half:], xp)
            late = late_log[pl.ds(h, 1), :]
            lc = logs[:, m * HD : m * HD + 1]
            gap0 = lc[0:half] - late[:, 0:half]
            gap1 = lc[half:] - late[:, half:]
            dec0 = jnp.exp(jnp.where(causal, gap0, -1e30))
            dec1 = jnp.concatenate(
                [
                    jnp.exp(lc[half:] - late[:, 0:half]),
                    jnp.exp(jnp.where(causal, gap1, -1e30)),
                ],
                axis=1,
            )
            m0 = dec0 * scores[0:half, 0:half]
            m1 = dec1 * scores[half:, :]
            ds[0:half, 0:half] += dec0 * q0
            ds[half:, :] += dec1 * q1
            p0 = m0 * q0
            p1 = m1 * q1
            rsum = jnp.concatenate(
                [jnp.sum(p0, axis=1, keepdims=True), jnp.sum(p1, axis=1, keepdims=True)], axis=0
            )
            rows[...] += jnp.where(lane == h, rsum, 0.0)
            csum1 = jnp.sum(p1, axis=0, keepdims=True)
            csum0 = jnp.sum(p0, axis=0, keepdims=True)
            col_ref[pl.ds(h, 1), :] = csum1 + jnp.concatenate(
                [csum0, jnp.zeros((1, half), f32)], axis=1
            )
            early = dot00(m0.astype(bf16), gm[0:half])
            late_part = dot00(m1.astype(bf16), gm[half:])
            total = total + late_part + jnp.concatenate(
                [early, jnp.zeros((half, 128), f32)], axis=0
            )
        du_ref[:, pl.ds(pl.multiple_of(i * 128, 128), 128)] = total
        return carry

    lax.fori_loop(0, H // 4, pair, 0)
    hi, mid, _ = split3(ds[...])
    hi = hi.astype(bf16)
    mid = mid.astype(bf16)
    sg_ref[:, :N] = before_ref[:, :N] + dot00(hi, c) + dot00(mid, c)
    sg_ref[:, N:] = before_ref[:, N:] + dot10(hi, b) + dot10(mid, b)
    cross_ref[...] = rows[...].T[0:H, :] - col_ref[...]


def token_kernel(
    core_ref, tok_ref, x_ref, g_ref, logit_ref, bias_ref,
    keep_ref, send_ref, sig_ref, skip_ref, turned,
):
    spread = head_rows(N)
    turned[...] = tok_ref[...].T
    for chip in range(CHIPS):
        mine = pl.multiple_of((2 * chip + core_ref[0]) * ROWS, 16)
        theirs = pl.multiple_of((2 * chip + 1 - core_ref[0]) * ROWS, 16)
        keep_ref[chip * ROWS : (chip + 1) * ROWS, :] = turned[pl.ds(mine, ROWS), :]
        send_ref[chip * ROWS : (chip + 1) * ROWS, :] = turned[pl.ds(theirs, ROWS), :].astype(f32)
    x = x_ref[...].astype(f32)
    g = g_ref[...].astype(f32)
    _, sig_ref[...] = step_sizes(logit_ref[...], bias_ref[...])
    part = jnp.sum((x * g).reshape(T // 8, 8, W), axis=0)
    skip = dot11(jnp.concatenate(split3(part), axis=0).astype(bf16), spread)
    skip = jnp.sum(skip, axis=0, keepdims=True)
    skip_ref[...] = jnp.broadcast_to(jnp.where(iota((1, 128), 1) < H, skip, 0.0), (8, 128))


def half_states(first, decay, chip_ref, extra):
    one = jnp.ones((1, W), f32)
    zero = jnp.zeros((1, W), f32)
    s = jnp.where(first, one, decay) * chip_ref[0:HALF, :] + jnp.where(first, zero, one) * extra
    e = jnp.where(first, decay, one) * chip_ref[HALF:N, :] + jnp.where(first, one, zero) * extra
    return s, e, jnp.sum((s * e).reshape(HALF // 8, 8, W), axis=0)


def near_kernel(core_ref, chip_ref, got_ref, xw_ref, ge_ref, s_ref, e_ref, meet_ref, part_ref, decay_ref):
    first = core_ref[0] == 0
    wide = widen_row(got_ref[0:8, W:], head_rows(N))[0:1]
    extra = jnp.where(first, got_ref[HALF:N, 0:W], got_ref[0:HALF, 0:W])
    decay_ref[...] = got_ref[0:8, W:]
    s, e, meet_ref[...] = half_states(first, wide, chip_ref, extra)
    s_ref[...] = s.astype(bf16)
    e_ref[...] = e.astype(bf16)
    part_ref[...] = jnp.concatenate(
        [dot11(xw_ref[...], e_ref[...]), dot11(ge_ref[...], s_ref[...])], axis=1
    )


def state_kernel(
    core_ref, chip_ref, more_ref, near_s_ref, near_e_ref, near_meet_ref, part_ref, decay_ref,
    xw_ref, ge_ref, sgin_ref,
    sg_ref, sgsend_ref, s_ref, e_ref, meet_ref,
):
    core = core_ref[0]
    first = core == 0
    wide = widen_row(decay_ref[...], head_rows(N))[0:1]
    s, e, meet = half_states(first, wide, chip_ref, more_ref[...])
    meet_ref[...] = near_meet_ref[...] + meet
    s = s.astype(bf16)
    e = e.astype(bf16)
    own = pl.ds(pl.multiple_of(core * HALF, HALF), HALF)
    other = pl.ds(pl.multiple_of(HALF - core * HALF, HALF), HALF)
    s_ref[own, :] = near_s_ref[...]
    e_ref[own, :] = near_e_ref[...]
    s_ref[other, :] = s
    e_ref[other, :] = e
    far = jnp.concatenate([dot11(xw_ref[...], e), dot11(ge_ref[...], s)], axis=1)
    near = part_ref[...]
    lo = jnp.where(first, near, far)
    hi = jnp.where(first, far, near)
    sg = sgin_ref[...] + jnp.concatenate(
        [lo[:, :HALF], hi[:, :HALF], lo[:, HALF:], hi[:, HALF:]], axis=1
    )
    sg = sg.astype(bf16)
    sg_ref[...] = sg
    sgsend_ref[...] = sg.astype(f32)


def own_weight_kernel(keep_ref, sg_ref, out_ref):
    out_ref[...] = dot10(keep_ref[...], sg_ref[...])


def weight_kernel(own_ref, got_ref, sggot_ref, param_ref, paramgot_ref, out_ref):
    out = own_ref[...] + dot10(got_ref[...].astype(bf16), sggot_ref[...].astype(bf16))
    out_ref[:, 0:ROWS, :] = out.reshape(CHIPS, ROWS, 2 * N)
    params = param_ref[...] + paramgot_ref[...]
    params = jnp.concatenate([params, jnp.zeros_like(params)], axis=1)
    out_ref[:, ROWS:PROWS, :] = jnp.broadcast_to(params[None], (CHIPS, 8, 2 * N))


def logit_kernel(
    s_ref, e_ref, meet_ref, x_ref, g_ref, bc_ref, log_ref, dt_ref, sig_ref, rate_ref,
    crossa_ref, crossb_ref, cola_ref, colb_ref, skip_ref,
    logit_ref, param_ref,
):
    spread = head_rows(N)
    b = bc_ref[:, :N]
    c = bc_ref[:, N:]
    log_decay = log_ref[...]
    dt = dt_ref[...]
    last = log_decay[:, T - 1 : T]
    pick = spread[0:48]
    eb = dot10(b, e_ref[...])

    def head_sums(v):
        hi = v.astype(bf16)
        return dot11(pick, hi)[0:H]

    v = jnp.exp(last - log_decay) * dt * head_sums(x_ref[...].astype(f32) * eb)
    from_start = dot10(c, s_ref[...])
    carry = jnp.exp(log_decay) * head_sums(g_ref[...].astype(f32) * from_start)
    meet = dot11(pick, jnp.concatenate(split3(meet_ref[...]), axis=0).astype(bf16))[0:H]
    through = jnp.sum(meet, axis=1, keepdims=True) * jnp.exp(last)
    row = iota((T, T), 0)
    col = iota((T, T), 1)
    log_grad = (
        through
        + over_positions(carry + crossa_ref[...] + crossb_ref[...], row >= col)
        + over_positions(v, row < col)
    )
    rate = jnp.exp(column(rate_ref[...], H))
    dt_grad = (cola_ref[...] + colb_ref[...] + v) / dt - rate * log_grad
    logit = dt_grad * sig_ref[...]
    logit_ref[...] = logit
    on_lane = iota((H, 128), 0) == iota((H, 128), 1)

    def as_row(colsum):
        return jnp.sum(jnp.where(on_lane, colsum, 0.0), axis=0, keepdims=True)

    rate_row = as_row(jnp.sum(-rate * dt * log_grad, axis=1, keepdims=True))
    bias_row = as_row(jnp.sum(logit, axis=1, keepdims=True))
    param_ref[...] = jnp.concatenate(
        [rate_row, bias_row, skip_ref[0:1, :], jnp.zeros((5, 128), f32)], axis=0
    )


def scan_grad_kernel(
    first, e_ref, g_ref, bc_ref, log_ref, dt_ref, direct_ref, du_ref, *rest
):
    spread = head_rows(N, first, W // 2)
    log_decay = log_ref[...]
    eb = dot10(bc_ref[:, :N], e_ref[...])
    to_end = widen(jnp.exp(log_decay[:, T - 1 : T] - log_decay) * dt_ref[...], spread)
    direct_row = jnp.broadcast_to(
        jnp.concatenate([direct_ref[...], jnp.zeros((1, 128 - H), f32)], axis=1), (8, 128)
    )
    direct = widen_row(direct_row, spread)[0:1]
    rest[-1][...] = (du_ref[...] + to_end * eb + direct * g_ref[...].astype(f32)).astype(bf16)


def mixer_kernel(sg_ref, proj_ref, mixer_ref):
    mixer_ref[...] = dot11(sg_ref[...], proj_ref[...]).astype(bf16)


def call(kernel, outs, scratch=(), smem=1, far=0, flops=0, moved=0, n_in=0, mib=32):
    vmem = pl.BlockSpec(memory_space=pltpu.VMEM)
    return pl.pallas_call(
        kernel,
        out_shape=[jax.ShapeDtypeStruct(s, d) for s, d in outs],
        in_specs=[pl.BlockSpec(memory_space=pltpu.SMEM)] * smem
        + [vmem] * n_in
        + [pl.BlockSpec(memory_space=pltpu.HBM)] * far,
        out_specs=[vmem] * len(outs),
        scratch_shapes=list(scratch),
        compiler_params=pltpu.CompilerParams(vmem_limit_bytes=mib * 1024 * 1024),
        cost_estimate=pl.CostEstimate(flops=flops, bytes_accessed=moved, transcendentals=0),
    )


def on_device(tokens, scan_input, logits, grads, proj, bias, rate_log, direct):
    tok, x, lg, g = tokens[0], scan_input[0], logits[0], grads[0]
    place = lax.axis_index("seq")
    core = lax.rem(place, 2).astype(jnp.int32).reshape(1)
    chip = lax.div(place, 2)
    back = (chip >= CHIPS // 2).astype(jnp.int32).reshape(1)
    bias_row = bias.reshape(1, H)
    rate_row = rate_log.reshape(1, H)
    direct_row = direct.reshape(1, H)
    swap = [(i, i ^ 1) for i in range(2 * CHIPS)]
    same_core = [[2 * i + k for i in range(CHIPS)] for k in range(2)]
    exchange = partial(
        lax.all_to_all, axis_name="seq", split_axis=0, concat_axis=0, axis_index_groups=same_core
    )

    bc, xw, ge, keep, send, more, log_decay, dt = call(
        summary_kernel,
        [
            ((T, 2 * N), bf16), ((T, W), bf16), ((T, W), bf16),
            ((N, W + TAIL), f32), ((N, W + TAIL), f32), ((HALF, W), f32),
            ((H, T), f32), ((H, T), f32),
        ],
        [
            pltpu.VMEM((H, T), f32), pltpu.VMEM((T, W), bf16), pltpu.VMEM((T, W), bf16),
            pltpu.VMEM((T, W), bf16), pltpu.VMEM((W, 2 * N), bf16), pltpu.VMEM((2 * N, W), f32),
            pltpu.SemaphoreType.DMA((5,)),
        ],
        n_in=2, far=5, flops=int(1e9), moved=int(1e7), mib=54,
    )(core, bias_row, rate_row, lg, tok, x, g, proj)
    got = lax.ppermute(send, "seq", swap)
    (chips,) = call(
        chip_kernel, [((N, W + TAIL), f32)], n_in=2, flops=int(1e7), moved=int(4e6), mib=8
    )(core, keep, got)
    chips, tok_b = lax.optimization_barrier((chips, tok))
    owned = exchange(chips.reshape(CHIPS, 8, W + TAIL))

    def within(first, dt, before):
        return call(
            partial(within_kernel, first),
            [((T, W // 2), f32), ((T, 2 * N), f32), ((H, T), f32), ((H, T), f32)],
            [
                pltpu.VMEM((T, W), f32), pltpu.VMEM((H, T), f32),
                pltpu.VMEM((T, T), f32), pltpu.VMEM((T, 128), f32),
            ],
            smem=0, n_in=6, flops=int(8e9), moved=int(5e6), mib=56,
        )(x, g, bc, log_decay, dt, before)

    du_a, sg_a, cross_a, col_a = within(0, dt, jnp.zeros((T, 2 * N), f32))
    tokt, tokt_send, sig, skip = call(
        token_kernel,
        [
            ((W // 2, T), bf16), ((W // 2, T), f32), ((H, T), f32), ((8, 128), f32),
        ],
        [pltpu.VMEM((W, T), bf16)],
        n_in=5, flops=int(3e9), moved=int(8e6), mib=56,
    )(core, tok_b, x, g, lg, bias_row)
    tokt_got = lax.ppermute(tokt_send, "seq", swap)
    more = lax.ppermute(more, "seq", swap)
    owned, col_a = lax.optimization_barrier((owned, col_a))
    (starts,) = call(
        scan_kernel, [((CHIPS, 8, W), f32)], [pltpu.VMEM((CHIPS, 8, W), f32)],
        n_in=1, flops=int(1e7), moved=int(3e6), mib=6,
    )(back, owned)
    returned = exchange(starts).reshape(N, W)
    _, more, tokt_got, dt_b = lax.optimization_barrier((starts, more, tokt_got, dt))
    du_b, sg_b, cross_b, col_b = within(H // 4, dt_b, sg_a)
    returned, sg_b = lax.optimization_barrier((returned, sg_b))
    returned_got = lax.ppermute(returned, "seq", swap)
    near_s, near_e, near_meet, near_part, decay = call(
        near_kernel,
        [((HALF, W), bf16), ((HALF, W), bf16), ((8, W), f32), ((T, N), f32), ((8, TAIL), f32)],
        n_in=4, flops=int(4e8), moved=int(6e6), mib=10,
    )(core, returned, got, xw, ge)
    sg, sg_send, s_all, e_all, meet = call(
        state_kernel,
        [
            ((T, 2 * N), bf16), ((T, 2 * N), f32), ((N, W), bf16), ((N, W), bf16), ((8, W), f32)
        ],
        n_in=10, flops=int(4e8), moved=int(6e6), mib=10,
    )(
        core, returned_got, more, near_s, near_e, near_meet, near_part, decay, xw, ge, sg_b
    )
    sg_got = lax.ppermute(sg_send, "seq", swap)
    logit_grad, params = call(
        logit_kernel, [((H, T), f32), ((8, 128), f32)], smem=0, n_in=15,
        flops=int(4e8), moved=int(4e6), mib=10,
    )(
        s_all, e_all, meet, x, g, bc, log_decay, dt, sig, rate_row,
        cross_a, cross_b, col_a, col_b, skip,
    )
    params_got = lax.ppermute(params, "seq", swap)
    (own_weights,) = call(
        own_weight_kernel, [((W // 2, 2 * N), f32)], smem=0, n_in=2,
        flops=int(2e8), moved=int(2e6), mib=6,
    )(tokt, sg)
    (weights,) = call(
        weight_kernel, [((CHIPS, PROWS, 2 * N), f32)], smem=0, n_in=5,
        flops=int(2e8), moved=int(4e6), mib=8,
    )(own_weights, tokt_got, sg_got, params, params_got)
    parts = exchange(weights)
    parts, e_late, sg_late = lax.optimization_barrier((parts, e_all, sg))
    scan_grad = ()
    for part, du in ((0, du_a), (1, du_b)):

        def whole(shape):
            return pl.BlockSpec(shape, lambda i: (0, 0))

        def half_of(rows, part=part):
            return pl.BlockSpec((rows, W // 2), lambda i: (0, part))

        scan_grad = (
            pl.pallas_call(
                partial(scan_grad_kernel, part * (W // 2)),
                grid=(1,),
                out_shape=jax.ShapeDtypeStruct((T, W), bf16),
                in_specs=[
                    half_of(N), half_of(T), whole((T, 2 * N)), whole((H, T)), whole((H, T)),
                    whole((1, H)), whole((T, W // 2)),
                ]
                + [pl.BlockSpec(memory_space=pl.ANY)] * part,
                out_specs=half_of(T),
                input_output_aliases={7: 0} if part else {},
                compiler_params=pltpu.CompilerParams(vmem_limit_bytes=56 * 1024 * 1024),
                cost_estimate=pl.CostEstimate(
                    flops=int(1e9), bytes_accessed=int(5e6), transcendentals=0
                ),
            )(e_late, g, bc, log_decay, dt, direct_row, du, *scan_grad),
        )
    (scan_grad,) = scan_grad
    (mixer_grad,) = call(
        mixer_kernel, [((T, W), bf16)], smem=0, n_in=2, flops=int(1e9), moved=int(3e6), mib=56,
    )(sg_late, proj)
    total = jnp.sum(parts, axis=0)
    for k in (1, 2, 4):
        total = total + lax.ppermute(total, "dp", [(i, i ^ k) for i in range(8)])
    total = total * (float(T * 2 * CHIPS * 8) ** -0.5)
    return (
        scan_grad[None],
        logit_grad[None],
        mixer_grad[None],
        total[0:ROWS],
        total[ROWS, 0:H],
        total[ROWS + 2, 0:H],
        total[ROWS + 1, 0:H],
    )


def solution(mesh):
    placed = (
        P("dp", "seq", None),
        P("dp", "seq", None),
        P("dp", None, "seq"),
        P("dp", "seq", None),
        P(),
        P(),
        P(),
        P(),
    )
    return jax.shard_map(
        on_device,
        mesh=mesh,
        in_specs=placed,
        out_specs=(
            P("dp", "seq", None),
            P("dp", None, "seq"),
            P("dp", "seq", None),
            P("seq", None),
            P(),
            P(),
            P(),
        ),
        check_vma=False,
    )
```

```python
from functools import partial

import jax
import jax.numpy as jnp
from jax import lax
from jax.sharding import PartitionSpec as P
import jax.experimental.pallas as pl
import jax.experimental.pallas.tpu as pltpu

f32 = jnp.float32
bf16 = jnp.bfloat16

T = 256
H = 40
HD = 64
W = 2560
N = 128
HALF = 64
TAIL = 128
CHIPS = 16
ROWS = 80
PROWS = 88


def iota(shape, dim):
    return lax.broadcasted_iota(jnp.int32, shape, dim)


def split3(v):
    hi = v.astype(bf16).astype(f32)
    rest = v - hi
    mid = rest.astype(bf16).astype(f32)
    return hi, mid, rest - mid


def dot00(a, b):
    return lax.dot_general(a, b, (((0,), (0,)), ((), ())), preferred_element_type=f32)


def dot11(a, b):
    return lax.dot_general(a, b, (((1,), (1,)), ((), ())), preferred_element_type=f32)


def dot10(a, b):
    return lax.dot_general(a, b, (((1,), (0,)), ((), ())), preferred_element_type=f32)


def head_rows(count, first=0, width=W):
    lane_head = (iota((count, width), 1) + first) >> 6
    row = iota((count, width), 0)
    hit = (lane_head == row) | (lane_head == row - H) | (lane_head == row - 2 * H)
    return jnp.where(hit, 1.0, 0.0).astype(bf16)


def widen(v, spread):
    parts = jnp.concatenate(split3(v) + (jnp.zeros((8, T), f32),), axis=0).astype(bf16)
    return dot00(parts, spread)


def widen_row(row, spread):
    parts = jnp.concatenate(split3(row) + (jnp.zeros((8, 128), f32),), axis=0).astype(bf16)
    lanes = iota(spread.shape, 0) < H
    once = jnp.where(lanes, spread.astype(f32), 0.0).astype(bf16)
    out = dot10(parts, once)
    return out[0:8] + out[8:16] + out[16:24]


def column(row, count):
    eye = iota((count, count), 0) == iota((count, count), 1)
    return jnp.sum(jnp.where(eye, row, 0.0), axis=1, keepdims=True)


def over_positions(v, keep):
    parts = jnp.concatenate(split3(v) + (jnp.zeros((8, T), f32),), axis=0).astype(bf16)
    out = dot10(parts, jnp.where(keep, 1.0, 0.0).astype(bf16))
    return out[0:H] + out[H : 2 * H] + out[2 * H : 3 * H]


def step_sizes(logits, bias_row):
    z = logits + column(bias_row, H)
    e = jnp.exp(-jnp.abs(z))
    r = e / (2.0 + e)
    r2 = r * r
    poly = 1.0 / 17.0
    for odd in (15, 13, 11, 9, 7, 5, 3):
        poly = poly * r2 + 1.0 / odd
    dt = jnp.maximum(z, 0.0) + 2.0 * (r + r * r2 * poly)
    sig = jnp.where(z >= 0.0, 1.0, e) / (1.0 + e)
    return dt, sig


def summary_kernel(
    core_ref, bias_ref, rate_ref, logit_hbm, tok_hbm, x_hbm, g_hbm, proj_hbm,
    bc_ref, xw_ref, ge_ref, keep_ref, send_ref, more_ref, log_ref, dt_ref,
    logit_ref, tok_ref, x_ref, g_ref, proj_ref, both, sem,
):
    pairs = (
        (logit_hbm, logit_ref), (tok_hbm, tok_ref), (proj_hbm, proj_ref), (x_hbm, x_ref), (g_hbm, g_ref)
    )
    copies = [pltpu.make_async_copy(a, b, sem.at[i]) for i, (a, b) in enumerate(pairs)]
    for copy in copies:
        copy.start()
    spread = head_rows(N)
    copies[0].wait()
    dt, _ = step_sizes(logit_ref[...], bias_ref[...])
    rate = jnp.exp(column(rate_ref[...], H))
    log_decay = over_positions(-rate * dt, iota((T, T), 0) <= iota((T, T), 1))
    last = log_decay[:, T - 1 : T]
    log_ref[...] = log_decay
    dt_ref[...] = dt
    to_end = widen(jnp.exp(last - log_decay) * dt, spread)
    from_start = widen(jnp.exp(log_decay), spread)
    copies[1].wait()
    copies[2].wait()
    bc = dot10(tok_ref[...], proj_ref[...]).astype(bf16)
    bc_ref[...] = bc
    copies[3].wait()
    copies[4].wait()
    xw = (x_ref[...].astype(f32) * to_end).astype(bf16)
    xw_ref[...] = xw
    ge = (g_ref[...].astype(f32) * from_start).astype(bf16)
    ge_ref[...] = ge
    both[0:N, :] = dot00(bc[:, :N], xw)
    both[N : 2 * N, :] = dot00(bc[:, N:], ge)
    mine = pl.multiple_of(core_ref[0] * HALF, HALF)
    theirs = pl.multiple_of(HALF - core_ref[0] * HALF, HALF)
    keep_ref[0:HALF, 0:W] = both[pl.ds(mine, HALF), :]
    keep_ref[HALF:N, 0:W] = both[pl.ds(N + mine, HALF), :]
    send_ref[0:HALF, 0:W] = both[pl.ds(theirs, HALF), :]
    send_ref[HALF:N, 0:W] = both[pl.ds(N + theirs, HALF), :]
    more_ref[...] = both[pl.ds(pl.multiple_of(core_ref[0] * (N + HALF), HALF), HALF), :]
    on_lane = iota((H, TAIL), 0) == iota((H, TAIL), 1)
    decay = jnp.exp(jnp.sum(jnp.where(on_lane, last, 0.0), axis=0, keepdims=True))
    decay = jnp.broadcast_to(decay, (N, TAIL))
    keep_ref[:, W:] = decay
    send_ref[:, W:] = decay


def chip_kernel(core_ref, keep_ref, got_ref, out_ref):
    spread = head_rows(N)
    decay_mine = keep_ref[0:8, W:]
    decay_their = got_ref[0:8, W:]
    wide_mine = widen_row(decay_mine, spread)[0:1]
    wide_their = widen_row(decay_their, spread)[0:1]
    first = core_ref[0] == 0
    one = jnp.ones((1, W), f32)
    a = jnp.where(first, wide_their, one)
    b = jnp.where(first, one, wide_mine)
    c = jnp.where(first, one, wide_their)
    d = jnp.where(first, wide_mine, one)
    out_ref[0:HALF, 0:W] = a * keep_ref[0:HALF, 0:W] + b * got_ref[0:HALF, 0:W]
    out_ref[HALF:N, 0:W] = c * keep_ref[HALF:N, 0:W] + d * got_ref[HALF:N, 0:W]
    out_ref[:, W:] = keep_ref[:, W:] * got_ref[:, W:]


def scan_kernel(back_ref, in_ref, out_ref, wide):
    spread = head_rows(N)
    for c in range(CHIPS):
        wide[c] = widen_row(in_ref[c, :, W:], spread)
    back = back_ref[0]
    state = jnp.zeros((8, W), f32)
    for i in range(CHIPS):
        c = jnp.where(back == 1, CHIPS - 1 - i, i)
        out_ref[c] = state
        state = wide[c] * state + in_ref[c, :, 0:W]


def within_kernel(
    first, x_ref, g_ref, bc_ref, log_ref, dt_ref, before_ref,
    du_ref, sg_ref, cross_ref, col_ref,
    wide_log, late_log, ds, rows,
):
    half = T // 2
    spread = head_rows(N)
    log_decay = log_ref[...]
    dt = dt_ref[...]
    wide_log[...] = widen(log_decay, spread)
    late_log[...] = log_decay - jnp.log(dt)
    b = bc_ref[:, :N]
    c = bc_ref[:, N:]
    scores = dot11(c, b)
    ds[...] = jnp.zeros((T, T), f32)
    rows[...] = jnp.zeros((T, 128), f32)
    col_ref[...] = jnp.zeros((H, T), f32)
    causal = iota((half, half), 0) >= iota((half, half), 1)
    lane = iota((T, 128), 1)

    def pair(i, carry):
        cols = pl.ds(pl.multiple_of((first + i) * 128, 128), 128)
        xp = x_ref[:, cols]
        gp = g_ref[:, cols]
        logs = wide_log[:, cols]
        total = jnp.zeros((T, 128), f32)
        for m in range(2):
            h = 2 * (first + i) + m
            gm = jnp.where((lane >= HD) == (m == 1), gp.astype(f32), 0.0).astype(bf16)
            q0 = dot11(gm[0:half], xp[0:half])
            q1 = dot11(gm[half:], xp)
            late = late_log[pl.ds(h, 1), :]
            lc = logs[:, m * HD : m * HD + 1]
            gap0 = lc[0:half] - late[:, 0:half]
            gap1 = lc[half:] - late[:, half:]
            dec0 = jnp.exp(jnp.where(causal, gap0, -1e30))
            dec1 = jnp.concatenate(
                [
                    jnp.exp(lc[half:] - late[:, 0:half]),
                    jnp.exp(jnp.where(causal, gap1, -1e30)),
                ],
                axis=1,
            )
            m0 = dec0 * scores[0:half, 0:half]
            m1 = dec1 * scores[half:, :]
            ds[0:half, 0:half] += dec0 * q0
            ds[half:, :] += dec1 * q1
            p0 = m0 * q0
            p1 = m1 * q1
            rsum = jnp.concatenate(
                [jnp.sum(p0, axis=1, keepdims=True), jnp.sum(p1, axis=1, keepdims=True)], axis=0
            )
            rows[...] += jnp.where(lane == h, rsum, 0.0)
            csum1 = jnp.sum(p1, axis=0, keepdims=True)
            csum0 = jnp.sum(p0, axis=0, keepdims=True)
            col_ref[pl.ds(h, 1), :] = csum1 + jnp.concatenate(
                [csum0, jnp.zeros((1, half), f32)], axis=1
            )
            early = dot00(m0.astype(bf16), gm[0:half])
            late_part = dot00(m1.astype(bf16), gm[half:])
            total = total + late_part + jnp.concatenate(
                [early, jnp.zeros((half, 128), f32)], axis=0
            )
        du_ref[:, pl.ds(pl.multiple_of(i * 128, 128), 128)] = total
        return carry

    lax.fori_loop(0, H // 4, pair, 0)
    hi, mid, _ = split3(ds[...])
    hi = hi.astype(bf16)
    mid = mid.astype(bf16)
    sg_ref[:, :N] = before_ref[:, :N] + dot00(hi, c) + dot00(mid, c)
    sg_ref[:, N:] = before_ref[:, N:] + dot10(hi, b) + dot10(mid, b)
    cross_ref[...] = rows[...].T[0:H, :] - col_ref[...]


def token_kernel(
    core_ref, tok_ref, x_ref, g_ref, logit_ref, bias_ref,
    keep_ref, send_ref, sig_ref, skip_ref, turned,
):
    spread = head_rows(N)
    turned[...] = tok_ref[...].T
    for chip in range(CHIPS):
        mine = pl.multiple_of((2 * chip + core_ref[0]) * ROWS, 16)
        theirs = pl.multiple_of((2 * chip + 1 - core_ref[0]) * ROWS, 16)
        keep_ref[chip * ROWS : (chip + 1) * ROWS, :] = turned[pl.ds(mine, ROWS), :]
        send_ref[chip * ROWS : (chip + 1) * ROWS, :] = turned[pl.ds(theirs, ROWS), :].astype(f32)
    x = x_ref[...].astype(f32)
    g = g_ref[...].astype(f32)
    _, sig_ref[...] = step_sizes(logit_ref[...], bias_ref[...])
    part = jnp.sum((x * g).reshape(T // 8, 8, W), axis=0)
    skip = dot11(jnp.concatenate(split3(part), axis=0).astype(bf16), spread)
    skip = jnp.sum(skip, axis=0, keepdims=True)
    skip_ref[...] = jnp.broadcast_to(jnp.where(iota((1, 128), 1) < H, skip, 0.0), (8, 128))


def half_states(first, decay, chip_ref, extra):
    one = jnp.ones((1, W), f32)
    zero = jnp.zeros((1, W), f32)
    s = jnp.where(first, one, decay) * chip_ref[0:HALF, :] + jnp.where(first, zero, one) * extra
    e = jnp.where(first, decay, one) * chip_ref[HALF:N, :] + jnp.where(first, one, zero) * extra
    return s, e, jnp.sum((s * e).reshape(HALF // 8, 8, W), axis=0)


def near_kernel(core_ref, chip_ref, got_ref, xw_ref, ge_ref, s_ref, e_ref, meet_ref, part_ref, decay_ref):
    first = core_ref[0] == 0
    wide = widen_row(got_ref[0:8, W:], head_rows(N))[0:1]
    extra = jnp.where(first, got_ref[HALF:N, 0:W], got_ref[0:HALF, 0:W])
    decay_ref[...] = got_ref[0:8, W:]
    s, e, meet_ref[...] = half_states(first, wide, chip_ref, extra)
    s_ref[...] = s.astype(bf16)
    e_ref[...] = e.astype(bf16)
    part_ref[...] = jnp.concatenate(
        [dot11(xw_ref[...], e_ref[...]), dot11(ge_ref[...], s_ref[...])], axis=1
    )


def state_kernel(
    core_ref, chip_ref, more_ref, near_s_ref, near_e_ref, near_meet_ref, part_ref, decay_ref,
    xw_ref, ge_ref, sgin_ref,
    sg_ref, sgsend_ref, s_ref, e_ref, meet_ref,
):
    core = core_ref[0]
    first = core == 0
    wide = widen_row(decay_ref[...], head_rows(N))[0:1]
    s, e, meet = half_states(first, wide, chip_ref, more_ref[...])
    meet_ref[...] = near_meet_ref[...] + meet
    s = s.astype(bf16)
    e = e.astype(bf16)
    own = pl.ds(pl.multiple_of(core * HALF, HALF), HALF)
    other = pl.ds(pl.multiple_of(HALF - core * HALF, HALF), HALF)
    s_ref[own, :] = near_s_ref[...]
    e_ref[own, :] = near_e_ref[...]
    s_ref[other, :] = s
    e_ref[other, :] = e
    far = jnp.concatenate([dot11(xw_ref[...], e), dot11(ge_ref[...], s)], axis=1)
    near = part_ref[...]
    lo = jnp.where(first, near, far)
    hi = jnp.where(first, far, near)
    sg = sgin_ref[...] + jnp.concatenate(
        [lo[:, :HALF], hi[:, :HALF], lo[:, HALF:], hi[:, HALF:]], axis=1
    )
    sg = sg.astype(bf16)
    sg_ref[...] = sg
    sgsend_ref[...] = sg.astype(f32)


def own_weight_kernel(keep_ref, sg_ref, out_ref):
    out_ref[...] = dot10(keep_ref[...], sg_ref[...])


def weight_kernel(own_ref, got_ref, sggot_ref, param_ref, paramgot_ref, out_ref):
    out = own_ref[...] + dot10(got_ref[...].astype(bf16), sggot_ref[...].astype(bf16))
    out_ref[:, 0:ROWS, :] = out.reshape(CHIPS, ROWS, 2 * N)
    params = param_ref[...] + paramgot_ref[...]
    params = jnp.concatenate([params, jnp.zeros_like(params)], axis=1)
    out_ref[:, ROWS:PROWS, :] = jnp.broadcast_to(params[None], (CHIPS, 8, 2 * N))


def logit_kernel(
    s_ref, e_ref, meet_ref, x_ref, g_ref, bc_ref, log_ref, dt_ref, sig_ref, rate_ref,
    crossa_ref, crossb_ref, cola_ref, colb_ref, skip_ref,
    logit_ref, param_ref,
):
    spread = head_rows(N)
    b = bc_ref[:, :N]
    c = bc_ref[:, N:]
    log_decay = log_ref[...]
    dt = dt_ref[...]
    last = log_decay[:, T - 1 : T]
    pick = spread[0:48]
    eb = dot10(b, e_ref[...])

    def head_sums(v):
        hi = v.astype(bf16)
        return dot11(pick, hi)[0:H]

    v = jnp.exp(last - log_decay) * dt * head_sums(x_ref[...].astype(f32) * eb)
    from_start = dot10(c, s_ref[...])
    carry = jnp.exp(log_decay) * head_sums(g_ref[...].astype(f32) * from_start)
    meet = dot11(pick, jnp.concatenate(split3(meet_ref[...]), axis=0).astype(bf16))[0:H]
    through = jnp.sum(meet, axis=1, keepdims=True) * jnp.exp(last)
    row = iota((T, T), 0)
    col = iota((T, T), 1)
    log_grad = (
        through
        + over_positions(carry + crossa_ref[...] + crossb_ref[...], row >= col)
        + over_positions(v, row < col)
    )
    rate = jnp.exp(column(rate_ref[...], H))
    dt_grad = (cola_ref[...] + colb_ref[...] + v) / dt - rate * log_grad
    logit = dt_grad * sig_ref[...]
    logit_ref[...] = logit
    on_lane = iota((H, 128), 0) == iota((H, 128), 1)

    def as_row(colsum):
        return jnp.sum(jnp.where(on_lane, colsum, 0.0), axis=0, keepdims=True)

    rate_row = as_row(jnp.sum(-rate * dt * log_grad, axis=1, keepdims=True))
    bias_row = as_row(jnp.sum(logit, axis=1, keepdims=True))
    param_ref[...] = jnp.concatenate(
        [rate_row, bias_row, skip_ref[0:1, :], jnp.zeros((5, 128), f32)], axis=0
    )


def scan_grad_kernel(
    first, e_ref, g_ref, bc_ref, log_ref, dt_ref, direct_ref, du_ref, *rest
):
    spread = head_rows(N, first, W // 2)
    log_decay = log_ref[...]
    eb = dot10(bc_ref[:, :N], e_ref[...])
    to_end = widen(jnp.exp(log_decay[:, T - 1 : T] - log_decay) * dt_ref[...], spread)
    direct_row = jnp.broadcast_to(
        jnp.concatenate([direct_ref[...], jnp.zeros((1, 128 - H), f32)], axis=1), (8, 128)
    )
    direct = widen_row(direct_row, spread)[0:1]
    rest[-1][...] = (du_ref[...] + to_end * eb + direct * g_ref[...].astype(f32)).astype(bf16)


def mixer_kernel(sg_ref, proj_ref, mixer_ref):
    mixer_ref[...] = dot11(sg_ref[...], proj_ref[...]).astype(bf16)


def call(kernel, outs, scratch=(), smem=1, far=0, flops=0, moved=0, n_in=0, mib=32):
    vmem = pl.BlockSpec(memory_space=pltpu.VMEM)
    return pl.pallas_call(
        kernel,
        out_shape=[jax.ShapeDtypeStruct(s, d) for s, d in outs],
        in_specs=[pl.BlockSpec(memory_space=pltpu.SMEM)] * smem
        + [vmem] * n_in
        + [pl.BlockSpec(memory_space=pltpu.HBM)] * far,
        out_specs=[vmem] * len(outs),
        scratch_shapes=list(scratch),
        compiler_params=pltpu.CompilerParams(vmem_limit_bytes=mib * 1024 * 1024),
        cost_estimate=pl.CostEstimate(flops=flops, bytes_accessed=moved, transcendentals=0),
    )


def on_device(tokens, scan_input, logits, grads, proj, bias, rate_log, direct):
    tok, x, lg, g = tokens[0], scan_input[0], logits[0], grads[0]
    place = lax.axis_index("seq")
    core = lax.rem(place, 2).astype(jnp.int32).reshape(1)
    chip = lax.div(place, 2)
    back = (chip >= CHIPS // 2).astype(jnp.int32).reshape(1)
    bias_row = bias.reshape(1, H)
    rate_row = rate_log.reshape(1, H)
    direct_row = direct.reshape(1, H)
    swap = [(i, i ^ 1) for i in range(2 * CHIPS)]
    same_core = [[2 * i + k for i in range(CHIPS)] for k in range(2)]
    exchange = partial(
        lax.all_to_all, axis_name="seq", split_axis=0, concat_axis=0, axis_index_groups=same_core
    )

    bc, xw, ge, keep, send, more, log_decay, dt = call(
        summary_kernel,
        [
            ((T, 2 * N), bf16), ((T, W), bf16), ((T, W), bf16),
            ((N, W + TAIL), f32), ((N, W + TAIL), f32), ((HALF, W), f32),
            ((H, T), f32), ((H, T), f32),
        ],
        [
            pltpu.VMEM((H, T), f32), pltpu.VMEM((T, W), bf16), pltpu.VMEM((T, W), bf16),
            pltpu.VMEM((T, W), bf16), pltpu.VMEM((W, 2 * N), bf16), pltpu.VMEM((2 * N, W), f32),
            pltpu.SemaphoreType.DMA((5,)),
        ],
        n_in=2, far=5, flops=int(1e9), moved=int(1e7), mib=54,
    )(core, bias_row, rate_row, lg, tok, x, g, proj)
    got = lax.ppermute(send, "seq", swap)
    (chips,) = call(
        chip_kernel, [((N, W + TAIL), f32)], n_in=2, flops=int(1e7), moved=int(4e6), mib=8
    )(core, keep, got)
    chips, tok_b = lax.optimization_barrier((chips, tok))
    owned = exchange(chips.reshape(CHIPS, 8, W + TAIL))

    def within(first, dt, before):
        return call(
            partial(within_kernel, first),
            [((T, W // 2), f32), ((T, 2 * N), f32), ((H, T), f32), ((H, T), f32)],
            [
                pltpu.VMEM((T, W), f32), pltpu.VMEM((H, T), f32),
                pltpu.VMEM((T, T), f32), pltpu.VMEM((T, 128), f32),
            ],
            smem=0, n_in=6, flops=int(8e9), moved=int(5e6), mib=56,
        )(x, g, bc, log_decay, dt, before)

    du_a, sg_a, cross_a, col_a = within(0, dt, jnp.zeros((T, 2 * N), f32))
    tokt, tokt_send, sig, skip = call(
        token_kernel,
        [
            ((W // 2, T), bf16), ((W // 2, T), f32), ((H, T), f32), ((8, 128), f32),
        ],
        [pltpu.VMEM((W, T), bf16)],
        n_in=5, flops=int(3e9), moved=int(8e6), mib=56,
    )(core, tok_b, x, g, lg, bias_row)
    tokt_got = lax.ppermute(tokt_send, "seq", swap)
    more = lax.ppermute(more, "seq", swap)
    owned, col_a = lax.optimization_barrier((owned, col_a))
    (starts,) = call(
        scan_kernel, [((CHIPS, 8, W), f32)], [pltpu.VMEM((CHIPS, 8, W), f32)],
        n_in=1, flops=int(1e7), moved=int(3e6), mib=6,
    )(back, owned)
    returned = exchange(starts).reshape(N, W)
    _, more, tokt_got, dt_b = lax.optimization_barrier((starts, more, tokt_got, dt))
    du_b, sg_b, cross_b, col_b = within(H // 4, dt_b, sg_a)
    returned, sg_b = lax.optimization_barrier((returned, sg_b))
    returned_got = lax.ppermute(returned, "seq", swap)
    near_s, near_e, near_meet, near_part, decay = call(
        near_kernel,
        [((HALF, W), bf16), ((HALF, W), bf16), ((8, W), f32), ((T, N), f32), ((8, TAIL), f32)],
        n_in=4, flops=int(4e8), moved=int(6e6), mib=10,
    )(core, returned, got, xw, ge)
    sg, sg_send, s_all, e_all, meet = call(
        state_kernel,
        [
            ((T, 2 * N), bf16), ((T, 2 * N), f32), ((N, W), bf16), ((N, W), bf16), ((8, W), f32)
        ],
        n_in=10, flops=int(4e8), moved=int(6e6), mib=10,
    )(
        core, returned_got, more, near_s, near_e, near_meet, near_part, decay, xw, ge, sg_b
    )
    sg_got = lax.ppermute(sg_send, "seq", swap)
    logit_grad, params = call(
        logit_kernel, [((H, T), f32), ((8, 128), f32)], smem=0, n_in=15,
        flops=int(4e8), moved=int(4e6), mib=10,
    )(
        s_all, e_all, meet, x, g, bc, log_decay, dt, sig, rate_row,
        cross_a, cross_b, col_a, col_b, skip,
    )
    params_got = lax.ppermute(params, "seq", swap)
    (own_weights,) = call(
        own_weight_kernel, [((W // 2, 2 * N), f32)], smem=0, n_in=2,
        flops=int(2e8), moved=int(2e6), mib=6,
    )(tokt, sg)
    (weights,) = call(
        weight_kernel, [((CHIPS, PROWS, 2 * N), f32)], smem=0, n_in=5,
        flops=int(2e8), moved=int(4e6), mib=8,
    )(own_weights, tokt_got, sg_got, params, params_got)
    parts = exchange(weights)
    parts, e_late, sg_late = lax.optimization_barrier((parts, e_all, sg))
    scan_grad = ()
    for part, du in ((0, du_a), (1, du_b)):

        def whole(shape):
            return pl.BlockSpec(shape, lambda i: (0, 0))

        def half_of(rows, part=part):
            return pl.BlockSpec((rows, W // 2), lambda i: (0, part))

        scan_grad = (
            pl.pallas_call(
                partial(scan_grad_kernel, part * (W // 2)),
                grid=(1,),
                out_shape=jax.ShapeDtypeStruct((T, W), bf16),
                in_specs=[
                    half_of(N), half_of(T), whole((T, 2 * N)), whole((H, T)), whole((H, T)),
                    whole((1, H)), whole((T, W // 2)),
                ]
                + [pl.BlockSpec(memory_space=pl.ANY)] * part,
                out_specs=half_of(T),
                input_output_aliases={7: 0} if part else {},
                compiler_params=pltpu.CompilerParams(vmem_limit_bytes=56 * 1024 * 1024),
                cost_estimate=pl.CostEstimate(
                    flops=int(1e9), bytes_accessed=int(5e6), transcendentals=0
                ),
            )(e_late, g, bc, log_decay, dt, direct_row, du, *scan_grad),
        )
    (scan_grad,) = scan_grad
    (mixer_grad,) = call(
        mixer_kernel, [((T, W), bf16)], smem=0, n_in=2, flops=int(1e9), moved=int(3e6), mib=56,
    )(sg_late, proj)
    total = jnp.sum(parts, axis=0)
    for k in (1, 2, 4):
        total = total + lax.ppermute(total, "dp", [(i, i ^ k) for i in range(8)])
    total = total * (float(T * 2 * CHIPS * 8) ** -0.5)
    return (
        scan_grad[None],
        logit_grad[None],
        mixer_grad[None],
        total[0:ROWS],
        total[ROWS, 0:H],
        total[ROWS + 2, 0:H],
        total[ROWS + 1, 0:H],
    )


def solution(mesh):
    placed = (
        P("dp", "seq", None),
        P("dp", "seq", None),
        P("dp", None, "seq"),
        P("dp", "seq", None),
        P(),
        P(),
        P(),
        P(),
    )
    return jax.shard_map(
        on_device,
        mesh=mesh,
        in_specs=placed,
        out_specs=(
            P("dp", "seq", None),
            P("dp", None, "seq"),
            P("dp", "seq", None),
            P("seq", None),
            P(),
            P(),
            P(),
        ),
        check_vma=False,
    )
```
